32 devices in a mesh: gz: 4 (over x, core), xy: 8 (over z, y).
Axes of the slice: x: 2, y: 2, z: 4, core: 2. Of those that a mesh axis runs over, the one named last changes fastest.
Arguments:
- parent_feat: bfloat16 [32, 64, 512], P(('gz', 'xy')), may hold values from -6 to 6
- parent_cell: int32 [32, 512], P(('gz', 'xy')), may hold values from 0 to 255
- send_count: int32 [32, 32], P(('gz', 'xy')), may hold values from 1 to 16, as said below
- up_weight: bfloat16 [8, 64, 64], replicated, may hold values from -0.75 to 0.75
- conv_one: bfloat16 [27, 64, 64], replicated, may hold values from -0.15625 to 0.15625
- conv_two: bfloat16 [27, 64, 64], replicated, may hold values from -0.15625 to 0.15625
- child_mask: int32 [16, 8, 512], P('xy', None, 'gz'), may hold values 0 or 1
- cotangent: bfloat16 [64, 16, 8, 512], P(None, 'xy', None, 'gz'), may hold values from -6 to 6
Outputs:
- decoded: bfloat16 [64, 16, 8, 512], P(None, 'xy', None, 'gz')
- grad_parent: bfloat16 [32, 64, 512], P(('gz', 'xy'))
- grad_one: float32 [27, 64, 64], replicated
- grad_two: float32 [27, 64, 64], replicated
- grad_up: float32 [8, 64, 64], replicated
The draws below stay inside these ranges and needn't reach their ends.
Inputs may be any that keep to these rules, and one draw needn't show every extreme that they name: `send_count`: some receiver gets 16 live slots from every sender, and every sender fills all 16 slots to some receiver. `parent_cell`: several slots may name the same parent voxel; their features add.
All inputs are finite; a program needn't handle non-finite values. No bound on the sum of `child_mask` on one device may be relied on, other than what follows from the above.
Results may differ from the reference program's by a relative error of at most 0.008.
Values may be sent and summed in bfloat16 or wider, within the bound.
A program may use at most 64 MiB of HBM per device.

```python
import math
import jax
import jax.numpy as jnp
from jax import lax

C = 64
CX = 2
CY = 8
CZ = 128
CAP = 16
XCELLS = 16
ZCELLS = 512
SLOTS = 512
PCELLS = 256
N_GZ = 4
N_XY = 8


def draw_send_count(key, part):
    devices_all = SLOTS // CAP
    key_base = jax.random.fold_in(key, 11)
    key_hot = jax.random.fold_in(key, 12)
    key_star = jax.random.fold_in(key, 13)
    base = jax.random.randint(key_base, (devices_all, devices_all), 1, CAP + 1)
    hot = jax.random.randint(key_hot, (devices_all,), 0, devices_all)
    star = jax.random.randint(key_star, (), 0, devices_all)
    target = jnp.arange(devices_all, dtype=jnp.int32)
    full = (target[None, :] == hot[:, None]) | (target[None, :] == star)
    return jnp.where(full, CAP, base).astype(jnp.int32)


def with_ends(array, stream_key, smallest, top_value):
    shape = array.shape
    place = [jax.random.randint(jax.random.fold_in(stream_key, axis), (), 0, shape[axis]) for axis in range(len(shape))]
    array = array.at[tuple(place)].set(smallest)
    longest = shape.index(max(shape))
    place[longest] = (place[longest] + 1) % shape[longest]
    return array.at[tuple(place)].set(top_value)


def steps_of(own_key, extent, cuts, smallest, largest):
    def one(dim, blocks):
        draws = jax.random.uniform(jax.random.fold_in(jax.random.fold_in(own_key, 6), dim), (blocks,), jnp.float32, smallest / len(cuts), largest / len(cuts))
        return jnp.repeat(jnp.exp(draws), extent[dim] // blocks).reshape((-1,) + (1,) * (len(extent) - dim - 1))

    factor_of = one(*cuts[0])
    for cut in cuts[1:]:
        factor_of = factor_of * one(*cut)
    return factor_of


def gaussian(key, dims, scale, limit, pieces=(), held_as=jnp.bfloat16):
    loudness = steps_of(key, dims, pieces, -0.22, 0.18) if pieces else 1.0
    values = jax.random.normal(key, dims, jnp.float32) * scale * loudness
    return jnp.minimum(jnp.maximum(values, -limit), limit).astype(held_as)


def setup_inputs(seed: int = 0) -> dict:
    key_list = jax.random.split(jax.random.key(seed), 9)
    return {
        "parent_feat": gaussian(key_list[0], (N_GZ * N_XY, C, SLOTS), 1.0, 6.0, ((0, 32),)),
        "parent_cell": with_ends(jax.random.randint(key_list[1], (N_GZ * N_XY, SLOTS), 0, PCELLS), jax.random.fold_in(key_list[1], 1), 0, PCELLS - 1).astype(jnp.int32),
        "send_count": draw_send_count(jax.random.fold_in(key_list[8], 71), 0),
        "up_weight": gaussian(key_list[3], (8, C, C), C ** -0.5, 0.75),
        "conv_one": gaussian(key_list[4], (27, C, C), (27 * C) ** -0.5, 0.15625),
        "conv_two": gaussian(key_list[5], (27, C, C), (27 * C) ** -0.5, 0.15625),
        "child_mask": with_ends((jax.random.randint(key_list[6], (XCELLS, CY, ZCELLS), 0, 4) < 3).astype(jnp.int32), jax.random.fold_in(key_list[6], 1), 0, 1),
        "cotangent": gaussian(key_list[7], (C, XCELLS, CY, ZCELLS), 1.0, 6.0, ((1, 8), (3, 4))),
    }


OFFSETS = [(a, b, c) for a in (-1, 0, 1) for b in (-1, 0, 1) for c in (-1, 0, 1)]

def window(padded, offset, direction, shape):
    nx, ny, nz = (shape[1], shape[2], shape[3])
    ox, oy, oz = (offset[0] * direction, offset[1] * direction, offset[2] * direction)
    part = padded[:, 1 + ox:1 + ox + nx, 1 + oy:1 + oy + ny, 1 + oz:1 + oz + nz]
    return part.reshape(shape[0], -1)

def pad_field(field):
    return jnp.pad(field.astype(jnp.float32), ((0, 0), (1, 1), (1, 1), (1, 1)))

def convolve(field, weights, direction):
    padded = pad_field(field)
    total = jnp.zeros((field.shape[0], field.shape[1] * field.shape[2] * field.shape[3]), jnp.float32)
    for index, offset in enumerate(OFFSETS):
        matrix = weights[index].astype(jnp.float32)
        if direction < 0:
            matrix = matrix.T
        total = total + jnp.dot(matrix, window(padded, offset, direction, field.shape), precision=lax.Precision.HIGHEST)
    return total.reshape(field.shape)

def weight_terms(delta, field):
    padded = pad_field(field)
    flat = delta.astype(jnp.float32).reshape(delta.shape[0], -1)
    terms = [jnp.dot(flat, window(padded, offset, 1, field.shape).T, precision=lax.Precision.HIGHEST) for offset in OFFSETS]
    return jnp.stack(terms)

def silu_slope(value):
    sig = jax.nn.sigmoid(value)
    return sig * (1.0 + value * (1.0 - sig))

def to_global(tiles):
    shaped = tiles.reshape(N_GZ, N_XY, C, CX, CY, CZ).transpose(2, 1, 3, 4, 0, 5)
    return shaped.reshape(C, XCELLS, CY, ZCELLS)

def to_tiles(field):
    shaped = field.reshape(C, N_XY, CX, CY, N_GZ, CZ).transpose(4, 1, 0, 2, 3, 5)
    return shaped.reshape(N_GZ * N_XY, C, CX, CY, CZ)

def reference(parent_feat, parent_cell, send_count, up_weight, conv_one, conv_two, child_mask, cotangent):
    devices_all = N_GZ * N_XY
    half_x, half_y, half_z = (CX // 2, CY // 2, CZ // 2)
    slot_pos = jnp.arange(SLOTS, dtype=jnp.int32) % CAP
    live = slot_pos[None, :] < jnp.repeat(send_count, CAP, axis=1)
    feats = jnp.where(live[:, None, :], parent_feat, jnp.zeros_like(parent_feat))
    recv_feat = feats.reshape(devices_all, C, devices_all, CAP).transpose(2, 1, 0, 3).reshape(devices_all, C, SLOTS)
    recv_cell = parent_cell.reshape(devices_all, devices_all, CAP).transpose(1, 0, 2).reshape(devices_all, SLOTS)
    cell_ids = jnp.arange(PCELLS, dtype=jnp.int32)

    def tile_grid(pair):
        feat_block, cell_block = pair
        onehot = (cell_block[:, None] == cell_ids[None, :]).astype(jnp.float32)
        return jnp.dot(feat_block.astype(jnp.float32), onehot, precision=lax.Precision.HIGHEST).astype(jnp.bfloat16)
    grids = lax.map(tile_grid, (recv_feat, recv_cell))
    up8 = jnp.einsum('ocd,ndq->nocq', up_weight.astype(jnp.float32), grids.astype(jnp.float32), precision=lax.Precision.HIGHEST)
    up_tiles = up8.reshape(devices_all, 2, 2, 2, C, half_x, half_y, half_z).transpose(0, 4, 5, 1, 6, 2, 7, 3)
    up = to_global(up_tiles.reshape(devices_all, C, CX, CY, CZ))
    maskf = child_mask.astype(jnp.float32)
    lifted = (maskf * up).astype(jnp.bfloat16)
    first_pre = convolve(lifted, conv_one, 1)
    first_act = (maskf * jax.nn.silu(first_pre)).astype(jnp.bfloat16)
    second_pre = convolve(first_act, conv_two, 1)
    decoded = (maskf * jax.nn.silu(second_pre)).astype(jnp.bfloat16)
    scale = 1.0 / math.sqrt(XCELLS * CY * ZCELLS)
    delta_two = (cotangent.astype(jnp.float32) * maskf * silu_slope(second_pre)).astype(jnp.bfloat16)
    grad_two = weight_terms(delta_two, first_act) * scale
    back_one = convolve(delta_two, conv_two, -1)
    delta_one = (back_one * maskf * silu_slope(first_pre)).astype(jnp.bfloat16)
    grad_one = weight_terms(delta_one, lifted) * scale
    delta_up = (convolve(delta_one, conv_one, -1) * maskf).astype(jnp.bfloat16)
    du_tiles = to_tiles(delta_up).reshape(devices_all, C, half_x, 2, half_y, 2, half_z, 2)
    du8 = du_tiles.transpose(0, 3, 5, 7, 1, 2, 4, 6).reshape(devices_all, 8, C, PCELLS).astype(jnp.float32)
    grad_up = jnp.einsum('nocq,ndq->ocd', du8, grids.astype(jnp.float32), precision=lax.Precision.HIGHEST) * scale
    delta_parent = jnp.einsum('ocd,nocq->ndq', up_weight.astype(jnp.float32), du8, precision=lax.Precision.HIGHEST).astype(jnp.bfloat16)

    def slot_grads(pair):
        grid_block, cell_block = pair
        return jnp.take(grid_block, cell_block, axis=1)
    per_receiver = lax.map(slot_grads, (delta_parent, recv_cell))
    per_sender = per_receiver.reshape(devices_all, C, devices_all, CAP).transpose(2, 1, 0, 3).reshape(devices_all, C, SLOTS)
    grad_parent = jnp.where(live[:, None, :], per_sender, jnp.zeros_like(per_sender))
    return (decoded, grad_parent, grad_one, grad_two, grad_up)
```

```python
import functools
import math

import jax
import jax.numpy as jnp
from jax import lax
from jax.experimental import pallas as pl
from jax.experimental.pallas import tpu as pltpu
from jax.sharding import PartitionSpec as P

MESH = pl.DeviceIdType.MESH
F32 = jnp.float32
BF16 = jnp.bfloat16
LANES = 128
SIDES = [(1, 0), (-1, 0), (-1, 1), (0, 1), (1, 1), (-1, -1), (0, -1), (1, -1)]


def dot(a, b):
    return jnp.dot(a, b, preferred_element_type=F32)


def dot_nt(a, b):
    return lax.dot_general(a, b, (((1,), (1,)), ((), ())), preferred_element_type=F32)


def dot_tn(a, b):
    return lax.dot_general(a, b, (((0,), (0,)), ((), ())), preferred_element_type=F32)


def all_kernel(
    dims,
    src, wup, w1, w2, mask, cot,
    dec, ret_out, g1_out, g2_out, gup_out,
    got, slot_grad, ret,
    a1, b1, a2, b2,
    planes, plane_in, tile_out, tile_in,
    s_lift, s_act, s_grad, acc, dpad, pre1,
    pack_a, wire_a, in_a, part_a, mid_a, inx_a, full_a,
    pack_b, wire_b, in_b, part_b, mid_b, inx_b, full_b,
    sem_to, sem_back, sem_halo, sem_ra, sem_rb,
):
    n_gz, n_xy, ch, ny = dims
    n_dev = n_gz * n_xy
    width = ny * LANES
    gz = lax.axis_index("gz")
    xy = lax.axis_index("xy")
    me = gz * n_xy + xy

    barrier = pltpu.get_barrier_semaphore()

    def greet(k, carry):
        to = lax.rem(me + k, n_dev)
        pl.semaphore_signal(
            barrier, inc=1, device_id=(to // n_xy, lax.rem(to, n_xy)), device_id_type=MESH
        )
        return carry

    lax.fori_loop(1, n_dev, greet, 0)

    def weights(i, carry):
        rows = pl.ds(pl.multiple_of(i * ch, ch), ch)
        for w, a, b in ((w1, a1, b1), (w2, a2, b2)):
            a[rows, :] = jnp.concatenate([w[3 * i + t] for t in range(3)], axis=1)
            b[rows, :] = jnp.concatenate(
                [w[26 - 3 * i - t].astype(F32).T.astype(BF16) for t in range(3)], axis=1
            )
        return carry

    def near(dx, dz):
        x, z = xy + dx, gz + dz
        there = (x >= 0) & (x < n_xy) & (z >= 0) & (z < n_gz)
        return there, (z, x)

    def landing(e, side):
        dx, dz = SIDES[side]
        return plane_in.at[e, side] if dz == 0 else tile_in.at[e, side - 2]

    def halo_copy(e, side):
        dx, dz = SIDES[side]
        there, target = near(dx, dz)
        if dz == 0:
            source = planes.at[e, 1 if dx > 0 else 0]
        else:
            source = tile_out.at[e, 1 if dz > 0 else 0]
        return there, pltpu.make_async_remote_copy(
            src_ref=source,
            dst_ref=landing(e, side),
            send_sem=sem_halo.at[0, e, side],
            recv_sem=sem_halo.at[1, e, side],
            device_id=target,
            device_id_type=MESH,
        )

    for side, (dx, dz) in enumerate(SIDES):
        has_source, _ = near(-dx, -dz)

        @pl.when(jnp.logical_not(has_source))
        def _():
            for e in range(4):
                ref = landing(e, side)
                ref[...] = jnp.zeros(ref.shape, BF16)

    dpad[...] = jnp.zeros(dpad.shape, BF16)
    pl.semaphore_wait(barrier, n_dev - 1)

    def to_copy(k):
        to = lax.rem(me + k, n_dev)
        return pltpu.make_async_remote_copy(
            src_ref=src.at[to],
            dst_ref=got.at[k],
            send_sem=sem_to.at[0, k],
            recv_sem=sem_to.at[1, k],
            device_id=(to // n_xy, lax.rem(to, n_xy)),
            device_id_type=MESH,
        )

    def back_copy(k):
        to = lax.rem(me + n_dev - k, n_dev)
        return pltpu.make_async_remote_copy(
            src_ref=slot_grad.at[k],
            dst_ref=ret.at[me],
            send_sem=sem_back.at[0, k],
            recv_sem=sem_back.at[1, k],
            device_id=(to // n_xy, lax.rem(to, n_xy)),
            device_id_type=MESH,
        )

    def each_device(action):
        def step(k, carry):
            action(k)
            return carry

        lax.fori_loop(1, n_dev, step, 0)

    each_device(lambda k: to_copy(k).start())
    got[0] = src[me]
    lax.fori_loop(0, 9, weights, 0)
    each_device(lambda k: to_copy(k).wait())

    slots = got.shape[0] * got.shape[1]
    listed = got[...].reshape(slots, LANES)
    half = 4 * LANES
    column = lax.broadcasted_iota(jnp.int32, (1, half), 1)
    owner = (column // LANES) * (LANES // 2) + lax.rem(column, LANES) // 2
    cells = listed[:, ch : ch + 1].astype(F32)
    hot = jnp.where(cells == owner.astype(F32), 1.0, 0.0).astype(BF16)
    grid_twice = dot_tn(listed, hot)[:ch]
    even = lax.rem(column, 2) == 0
    none = jnp.zeros_like(grid_twice)
    parents = jnp.concatenate(
        [jnp.where(even, grid_twice, none), jnp.where(even, none, grid_twice)], axis=0
    ).astype(BF16)
    up = dot(wup[...], parents)

    lane = lax.broadcasted_iota(jnp.int32, (1, LANES), 1)

    def block(value, y):
        return value[:, y * LANES : (y + 1) * LANES]

    def plane_mask(x):
        return mask[:, x * width : (x + 1) * width]

    def send_halo(e, fields):
        edge = lax.rem(lane, 16)
        first = jnp.zeros((ch, LANES), F32)
        last = jnp.zeros((ch, LANES), F32)
        for x in range(2):
            planes[e, x] = fields[x]
        for side in (0, 1):
            there, copy = halo_copy(e, side)
            pl.when(there)(copy.start)
        for x in range(2):
            wide = fields[x].astype(F32)
            for y in range(ny):
                here = edge == (8 + x * 8 + y) % 16
                part = block(wide, y)
                first = jnp.where(here, part[:, :1], first)
                last = jnp.where(here, part[:, LANES - 1 :], last)
        tile_out[e, 0] = first.astype(BF16)
        tile_out[e, 1] = last.astype(BF16)
        for side in range(2, 8):
            there, copy = halo_copy(e, side)
            pl.when(there)(copy.start)

    def spread(e, fields, into):
        for side, (dx, dz) in enumerate(SIDES):
            has_source, _ = near(-dx, -dz)
            _, copy = halo_copy(e, side)
            pl.when(has_source)(copy.wait_recv)

        def edges(base):
            after, same, before = [tile_in[e, base + t].astype(F32) for t in range(3)]
            return jnp.where(lane < 8, before, jnp.where(lane < 24, same, after))

        low, high = edges(0), edges(3)
        for xp in range(4):
            if xp in (1, 2):
                field = fields[xp - 1]
            else:
                field = plane_in[e, 0 if xp == 0 else 1]
            wide = field.astype(F32)
            into[xp, ch : 2 * ch, :] = field
            for y in range(ny):
                part = block(wide, y)
                at = xp * 8 + y
                left = jnp.where(lane == 0, low[:, at : at + 1], pltpu.roll(part, 1, 1))
                right = jnp.where(
                    lane == LANES - 1, high[:, at : at + 1], pltpu.roll(part, LANES - 1, 1)
                )
                cols = slice(y * LANES, (y + 1) * LANES)
                into[xp, 0:ch, cols] = left.astype(BF16)
                into[xp, 2 * ch : 3 * ch, cols] = right.astype(BF16)

    REACH = [(-1,), (-1, 0), (0, 1), (1,)]

    def conv(matrix, held):
        acc[...] = jnp.zeros(acc.shape, F32)
        for xp in range(4):
            steps = REACH[xp]
            low = 3 * ch * (steps[0] + 1)
            product = dot(matrix[low : low + 3 * ch * len(steps), :], held[xp])
            for n, ox in enumerate(steps):
                x = xp - 1 - ox
                for oy in (-1, 0, 1):
                    row = (3 * n + oy + 1) * ch
                    cols = slice((1 - oy) * LANES, (1 - oy) * LANES + width)
                    acc[x, :, cols] += product[row : row + ch]
        return [acc[x, :, LANES : LANES + width] for x in range(2)]

    def tap_sums(deltas, held):
        for x in range(2):
            dpad[x, :, LANES : LANES + width] = deltas[x]
        total = [jnp.zeros((3 * ch, 3 * ch), F32) for _ in range(3)]
        for xp in range(4):
            steps = REACH[xp]
            rows = [
                dpad[xp - 1 - ox, :, (1 - oy) * LANES : (1 - oy) * LANES + width]
                for ox in steps
                for oy in (-1, 0, 1)
            ]
            product = dot_nt(jnp.concatenate(rows, axis=0), held[xp])
            for n, ox in enumerate(steps):
                total[ox + 1] = total[ox + 1] + product[3 * ch * n : 3 * ch * (n + 1)]
        return [total[i // 3][(i % 3) * ch : (i % 3 + 1) * ch] for i in range(9)]

    def pack_taps(taps, pack):
        for i in range(9):
            pack[i * ch : (i + 1) * ch, :] = taps[i][:, :LANES]
        for i in range(5):
            second = taps[2 * i + 1][:, LANES:] if i < 4 else jnp.zeros((ch, ch), F32)
            row = (9 + i) * ch
            pack[row : row + ch, :] = jnp.concatenate([taps[2 * i][:, LANES:], second], axis=1)

    def unpack_taps(full, out):
        for i in range(9):
            tile = full[i * ch : (i + 1) * ch]
            out[3 * i] = tile[:, :ch]
            out[3 * i + 1] = tile[:, ch:]
            pair = full[(9 + i // 2) * ch : (10 + i // 2) * ch]
            out[3 * i + 2] = pair[:, :ch] if i % 2 == 0 else pair[:, ch:]

    class Reduce:
        def __init__(self, pack, wire, in_gz, part, mid, in_xy, full, sems):
            self.pack, self.wire, self.in_gz, self.part = pack, wire, in_gz, part
            self.mid, self.in_xy, self.full, self.sems = mid, in_xy, full, sems
            self.rows = pack.shape[0] // n_gz
            self.sub = self.rows // n_xy

        def copies(self, phase):
            result = []
            for k in range(1, n_gz if phase in (0, 3) else n_xy):
                if phase in (0, 3):
                    to = lax.rem(gz + k, n_gz)
                    target = (to, xy)
                else:
                    to = lax.rem(xy + k, n_xy)
                    target = (gz, to)
                source, landed = [
                    lambda: (self.wire.at[to], self.in_gz.at[k - 1]),
                    lambda: (self.mid.at[to], self.in_xy.at[k - 1]),
                    lambda: (self.full.at[gz, xy], self.full.at[gz, xy]),
                    lambda: (self.full.at[gz], self.full.at[gz]),
                ][phase]()
                result.append(
                    pltpu.make_async_remote_copy(
                        src_ref=source,
                        dst_ref=landed,
                        send_sem=self.sems.at[0, phase, k - 1],
                        recv_sem=self.sems.at[1, phase, k - 1],
                        device_id=target,
                        device_id_type=MESH,
                    )
                )
            return result

        def start(self, phase):
            for copy in self.copies(phase):
                copy.start()

        def finish(self, phase):
            for copy in self.copies(phase):
                copy.wait()

        def begin(self):
            for g in range(n_gz):
                self.wire[g] = self.pack[g * self.rows : (g + 1) * self.rows].astype(BF16)
            self.start(0)

        def second(self):
            self.finish(0)
            total = self.pack[pl.ds(pl.multiple_of(gz * self.rows, 16), self.rows), :]
            for k in range(n_gz - 1):
                total = total + self.in_gz[k].astype(F32)
            for j in range(n_xy):
                piece = total[j * self.sub : (j + 1) * self.sub]
                self.part[j] = piece
                self.mid[j] = piece.astype(BF16)
            self.start(1)

        def third(self):
            self.finish(1)
            total = self.part[xy]
            for k in range(n_xy - 1):
                total = total + self.in_xy[k].astype(F32)
            self.full[gz, xy] = total.astype(BF16)
            self.start(2)

        def fourth(self):
            self.finish(2)
            self.start(3)

        def done(self):
            self.finish(3)
            return self.full[...].astype(F32).reshape(self.rows * n_gz, LANES)

    sum_a = Reduce(pack_a, wire_a, in_a, part_a, mid_a, inx_a, full_a, sem_ra)
    sum_b = Reduce(pack_b, wire_b, in_b, part_b, mid_b, inx_b, full_b, sem_rb)

    lifted = []
    for a in range(2):
        pieces = []
        for y in range(ny):
            j, b = y // 2, y % 2
            row = (2 * a + b) * ch
            pieces.append(up[row : row + ch, j * LANES : (j + 1) * LANES])
        lifted.append((jnp.concatenate(pieces, axis=1) * plane_mask(a)).astype(BF16))
    send_halo(0, lifted)
    spread(0, lifted, s_lift)
    first = conv(a1, s_lift)
    acts = []
    for x in range(2):
        pre1[x] = first[x]
        acts.append((plane_mask(x) * first[x] * jax.nn.sigmoid(first[x])).astype(BF16))
    send_halo(1, acts)
    spread(1, acts, s_act)
    second = conv(a2, s_act)
    deltas = []
    for x in range(2):
        v = second[x]
        sig = jax.nn.sigmoid(v)
        m = plane_mask(x)
        dec[:, x * width : (x + 1) * width] = (m * (v * sig)).astype(BF16)
        slope = sig * (1.0 + v * (1.0 - sig))
        deltas.append((cot[:, x * width : (x + 1) * width].astype(F32) * m * slope).astype(BF16))

    send_halo(2, deltas)
    taps_two = tap_sums(deltas, s_act)
    pack_taps(taps_two, pack_a)
    used = 14 * ch
    pack_a[used:, :] = jnp.zeros((pack_a.shape[0] - used, LANES), F32)
    sum_a.begin()
    spread(2, deltas, s_grad)
    back = conv(b2, s_grad)
    deltas = []
    for x in range(2):
        v = pre1[x]
        sig = jax.nn.sigmoid(v)
        slope = sig * (1.0 + v * (1.0 - sig))
        deltas.append((back[x] * plane_mask(x) * slope).astype(BF16))
    send_halo(3, deltas)
    pack_taps(tap_sums(deltas, s_lift), pack_b)
    sum_a.second()
    spread(3, deltas, s_grad)
    back = conv(b1, s_grad)
    du = [(back[x] * plane_mask(x)).astype(BF16) for x in range(2)]
    stacked = jnp.concatenate(
        [
            jnp.concatenate([block(du[a], 2 * j + b) for j in range(ny // 2)], axis=1)
            for a in range(2)
            for b in range(2)
        ],
        axis=0,
    )
    pack_b[used : used + 4 * ch, :] = dot_nt(stacked, parents)
    rest = used + 4 * ch
    if pack_b.shape[0] > rest:
        pack_b[rest:, :] = jnp.zeros((pack_b.shape[0] - rest, LANES), F32)
    sum_b.begin()
    by_parity = dot_tn(wup[...], stacked)
    kept = jnp.where(even, by_parity[:ch], by_parity[ch:])
    paired = kept + pltpu.roll(kept, half - 1, 1)
    parent_grad = jnp.where(even, paired, jnp.zeros_like(paired)).astype(BF16)
    wide_grad = jnp.concatenate([parent_grad, jnp.zeros_like(parent_grad)], axis=0)
    slot_grad[...] = dot_nt(hot, wide_grad).astype(BF16).reshape(slot_grad.shape)
    each_device(lambda k: back_copy(k).start())
    ret[me] = slot_grad[0]
    sum_a.third()
    sum_b.second()
    sum_a.fourth()
    sum_b.third()
    each_device(lambda k: back_copy(k).wait())
    ret_out[...] = ret[...].reshape(slots, LANES).astype(F32).T[:ch].astype(BF16)
    unpack_taps(sum_a.done(), g2_out)
    sum_b.fourth()
    last = sum_b.done()
    unpack_taps(last, g1_out)
    for p in range(4):
        tile = last[used + p * ch : used + (p + 1) * ch]
        gup_out[2 * p] = tile[:, :ch]
        gup_out[2 * p + 1] = tile[:, ch:]
    for e in range(4):
        for side in range(8):
            there, copy = halo_copy(e, side)
            pl.when(there)(copy.wait_send)


def local(
    parent_feat, parent_cell, send_count, up_weight, conv_one, conv_two, child_mask, cotangent
):
    ch, size_x, ny, size_z = cotangent.shape
    n_gz, n_xy = lax.axis_size("gz"), lax.axis_size("xy")
    n_dev = n_gz * n_xy
    slot_total = parent_feat.shape[2]
    cap = slot_total // n_dev
    voxels = size_x * ny * size_z
    width = ny * size_z
    live = (jnp.arange(cap, dtype=jnp.int32)[None, :] < send_count[0][:, None]).reshape(slot_total)
    feats = jnp.where(live[None, :], parent_feat[0], jnp.zeros_like(parent_feat[0]))
    src = jnp.concatenate(
        [feats, parent_cell.astype(BF16), jnp.zeros((LANES - ch - 1, slot_total), BF16)], axis=0
    ).T.reshape(n_dev, cap, LANES)
    wup = up_weight.reshape(4, 2, ch, ch).transpose(0, 2, 1, 3).reshape(4 * ch, 2 * ch)
    mask = child_mask.astype(F32).reshape(1, voxels)
    cot = cotangent.reshape(ch, voxels)
    unit = n_dev * 16
    rows_a = -(-14 * ch // unit) * unit
    rows_b = -(-18 * ch // unit) * unit

    def reduce_scratch(rows):
        per = rows // n_gz
        sub = per // n_xy
        return [
            pltpu.VMEM((rows, LANES), F32),
            pltpu.VMEM((n_gz, per, LANES), BF16),
            pltpu.VMEM((n_gz - 1, per, LANES), BF16),
            pltpu.VMEM((n_xy, sub, LANES), F32),
            pltpu.VMEM((n_xy, sub, LANES), BF16),
            pltpu.VMEM((n_xy - 1, sub, LANES), BF16),
            pltpu.VMEM((n_gz, n_xy, sub, LANES), BF16),
        ]

    vmem = pl.BlockSpec(memory_space=pltpu.VMEM)
    most = max(n_gz, n_xy) - 1
    dma = pltpu.SemaphoreType.DMA
    dec, ret, g1, g2, gup = pl.pallas_call(
        functools.partial(all_kernel, (n_gz, n_xy, ch, ny)),
        out_shape=(
            jax.ShapeDtypeStruct((ch, voxels), BF16),
            jax.ShapeDtypeStruct((ch, slot_total), BF16),
            jax.ShapeDtypeStruct((27, ch, ch), F32),
            jax.ShapeDtypeStruct((27, ch, ch), F32),
            jax.ShapeDtypeStruct((8, ch, ch), F32),
        ),
        in_specs=[vmem] * 6,
        out_specs=(vmem,) * 5,
        scratch_shapes=[
            pltpu.VMEM((n_dev, cap, LANES), BF16),
            pltpu.VMEM((n_dev, cap, LANES), BF16),
            pltpu.VMEM((n_dev, cap, LANES), BF16),
            pltpu.VMEM((9 * ch, 3 * ch), BF16),
            pltpu.VMEM((9 * ch, 3 * ch), BF16),
            pltpu.VMEM((9 * ch, 3 * ch), BF16),
            pltpu.VMEM((9 * ch, 3 * ch), BF16),
            pltpu.VMEM((4, 2, ch, width), BF16),
            pltpu.VMEM((4, 2, ch, width), BF16),
            pltpu.VMEM((4, 2, ch, LANES), BF16),
            pltpu.VMEM((4, 6, ch, LANES), BF16),
            pltpu.VMEM((4, 3 * ch, width), BF16),
            pltpu.VMEM((4, 3 * ch, width), BF16),
            pltpu.VMEM((4, 3 * ch, width), BF16),
            pltpu.VMEM((2, ch, width + 2 * LANES), F32),
            pltpu.VMEM((2, ch, width + 2 * LANES), BF16),
            pltpu.VMEM((2, ch, width), F32),
            *reduce_scratch(rows_a),
            *reduce_scratch(rows_b),
            dma((2, n_dev)),
            dma((2, n_dev)),
            dma((2, 4, 8)),
            dma((2, 4, most)),
            dma((2, 4, most)),
        ],
        compiler_params=pltpu.CompilerParams(
            collective_id=0, has_side_effects=True, vmem_limit_bytes=56 * 1024 * 1024
        ),
    )(src, wup, conv_one, conv_two, mask, cot)
    decoded = dec.reshape(cotangent.shape)
    grad_parent = jnp.where(live[None, :], ret, jnp.zeros_like(ret))[None]
    scale = 1.0 / math.sqrt(size_x * n_xy * ny * size_z * n_gz)
    return (decoded, grad_parent, g1 * scale, g2 * scale, gup * scale)


def solution(mesh):
    placed = (
        P(("gz", "xy"), None, None),
        P(("gz", "xy"), None),
        P(("gz", "xy"), None),
        P(),
        P(),
        P(),
        P("xy", None, "gz"),
        P(None, "xy", None, "gz"),
    )
    return jax.shard_map(
        local,
        mesh=mesh,
        in_specs=placed,
        out_specs=(P(None, "xy", None, "gz"), P(("gz", "xy"), None, None), P(), P(), P()),
        check_vma=False,
    )
```

```python
import functools
import math

import jax
import jax.numpy as jnp
from jax import lax
from jax.experimental import pallas as pl
from jax.experimental.pallas import tpu as pltpu
from jax.sharding import PartitionSpec as P

MESH = pl.DeviceIdType.MESH
F32 = jnp.float32
BF16 = jnp.bfloat16
LANES = 128
SIDES = [(1, 0), (-1, 0), (-1, 1), (0, 1), (1, 1), (-1, -1), (0, -1), (1, -1)]


def dot(a, b):
    return jnp.dot(a, b, preferred_element_type=F32)


def dot_nt(a, b):
    return lax.dot_general(a, b, (((1,), (1,)), ((), ())), preferred_element_type=F32)


def dot_tn(a, b):
    return lax.dot_general(a, b, (((0,), (0,)), ((), ())), preferred_element_type=F32)


def all_kernel(
    dims,
    feat, cell, count, w_up, w1, w2, mask_in, cot_in,
    dec, ret_out, out_a, out_b,
    src, wup, got, slot_grad, ret,
    a1, b1, a2, b2,
    planes, plane_in, tile_out, tile_in,
    s_lift, s_act, s_grad, acc, dpad, pre1,
    pack_a, wire_a, in_a, part_a, mid_a, inx_a, full_a,
    pack_b, wire_b, in_b, part_b, mid_b, inx_b, full_b,
    sem_to, sem_back, sem_halo, sem_ra, sem_rb,
):
    n_gz, n_xy, ch, ny = dims
    n_dev = n_gz * n_xy
    width = ny * LANES
    gz = lax.axis_index("gz")
    xy = lax.axis_index("xy")
    me = gz * n_xy + xy

    barrier = pltpu.get_barrier_semaphore()

    def greet(k, carry):
        to = lax.rem(me + k, n_dev)
        pl.semaphore_signal(
            barrier, inc=1, device_id=(to // n_xy, lax.rem(to, n_xy)), device_id_type=MESH
        )
        return carry

    lax.fori_loop(1, n_dev, greet, 0)

    def weights(i, carry):
        rows = pl.ds(pl.multiple_of(i * ch, ch), ch)
        for w, a, b in ((w1, a1, b1), (w2, a2, b2)):
            a[rows, :] = jnp.concatenate([w[3 * i + t] for t in range(3)], axis=1)
            b[rows, :] = jnp.concatenate(
                [w[26 - 3 * i - t].astype(F32).T.astype(BF16) for t in range(3)], axis=1
            )
        return carry

    def near(dx, dz):
        x, z = xy + dx, gz + dz
        there = (x >= 0) & (x < n_xy) & (z >= 0) & (z < n_gz)
        return there, (z, x)

    def landing(e, side):
        dx, dz = SIDES[side]
        return plane_in.at[e, side] if dz == 0 else tile_in.at[e, side - 2]

    def halo_copy(e, side):
        dx, dz = SIDES[side]
        there, target = near(dx, dz)
        if dz == 0:
            source = planes.at[e, 1 if dx > 0 else 0]
        else:
            source = tile_out.at[e, 1 if dz > 0 else 0]
        return there, pltpu.make_async_remote_copy(
            src_ref=source,
            dst_ref=landing(e, side),
            send_sem=sem_halo.at[0, e, side],
            recv_sem=sem_halo.at[1, e, side],
            device_id=target,
            device_id_type=MESH,
        )

    for side, (dx, dz) in enumerate(SIDES):
        has_source, _ = near(-dx, -dz)

        @pl.when(jnp.logical_not(has_source))
        def _():
            for e in range(4):
                ref = landing(e, side)
                ref[...] = jnp.zeros(ref.shape, BF16)

    dpad[...] = jnp.zeros(dpad.shape, BF16)
    slots = got.shape[0] * got.shape[1]
    cap = got.shape[1]
    slot = lax.broadcasted_iota(jnp.int32, (1, slots), 1)
    to_slot = lax.broadcasted_iota(jnp.int32, (n_dev, slots), 0) == slot // cap
    counts = jnp.broadcast_to(count[...].astype(F32), (8, n_dev)).astype(BF16)
    counts = dot(counts, jnp.where(to_slot, 1.0, 0.0).astype(BF16))[:1]
    live = lax.rem(slot, cap).astype(F32) < counts
    sent = jnp.concatenate(
        [
            jnp.where(live, feat[0].astype(F32), 0.0),
            jnp.broadcast_to(cell[...].astype(F32), (8, slots)),
            jnp.zeros((LANES - ch - 8, slots), F32),
        ],
        axis=0,
    )
    src[...] = sent.T.astype(BF16).reshape(src.shape)
    for i in range(4):
        wup[i * ch : (i + 1) * ch, :] = jnp.concatenate([w_up[2 * i], w_up[2 * i + 1]], axis=1)
    pl.semaphore_wait(barrier, n_dev - 1)

    def to_copy(k):
        to = lax.rem(me + k, n_dev)
        return pltpu.make_async_remote_copy(
            src_ref=src.at[to],
            dst_ref=got.at[k],
            send_sem=sem_to.at[0, k],
            recv_sem=sem_to.at[1, k],
            device_id=(to // n_xy, lax.rem(to, n_xy)),
            device_id_type=MESH,
        )

    def back_copy(k):
        to = lax.rem(me + n_dev - k, n_dev)
        return pltpu.make_async_remote_copy(
            src_ref=slot_grad.at[k],
            dst_ref=ret.at[me],
            send_sem=sem_back.at[0, k],
            recv_sem=sem_back.at[1, k],
            device_id=(to // n_xy, lax.rem(to, n_xy)),
            device_id_type=MESH,
        )

    def each_device(action):
        def step(k, carry):
            action(k)
            return carry

        lax.fori_loop(1, n_dev, step, 0)

    each_device(lambda k: to_copy(k).start())
    got[0] = src[me]
    lax.fori_loop(0, 9, weights, 0)
    each_device(lambda k: to_copy(k).wait())

    listed = got[...].reshape(slots, LANES)
    half = 4 * LANES
    column = lax.broadcasted_iota(jnp.int32, (1, half), 1)
    owner = (column // LANES) * (LANES // 2) + lax.rem(column, LANES) // 2
    cells = listed[:, ch : ch + 1].astype(F32)
    hot = jnp.where(cells == owner.astype(F32), 1.0, 0.0).astype(BF16)
    grid_twice = dot_tn(listed, hot)[:ch]
    even = lax.rem(column, 2) == 0
    none = jnp.zeros_like(grid_twice)
    parents = jnp.concatenate(
        [jnp.where(even, grid_twice, none), jnp.where(even, none, grid_twice)], axis=0
    ).astype(BF16)
    up = dot(wup[...], parents)

    lane = lax.broadcasted_iota(jnp.int32, (1, LANES), 1)

    def block(value, y):
        return value[:, y * LANES : (y + 1) * LANES]

    def plane_mask(x):
        rows = mask_in[x].astype(F32)
        return jnp.concatenate([rows[y : y + 1] for y in range(ny)], axis=1)

    def cot_plane(x):
        return cot_in[:, x].astype(F32).reshape(ch, width)

    def send_halo(e, fields):
        edge = lax.rem(lane, 16)
        first = jnp.zeros((ch, LANES), F32)
        last = jnp.zeros((ch, LANES), F32)
        for x in range(2):
            planes[e, x] = fields[x]
        for side in (0, 1):
            there, copy = halo_copy(e, side)
            pl.when(there)(copy.start)
        for x in range(2):
            wide = fields[x].astype(F32)
            for y in range(ny):
                here = edge == (8 + x * 8 + y) % 16
                part = block(wide, y)
                first = jnp.where(here, part[:, :1], first)
                last = jnp.where(here, part[:, LANES - 1 :], last)
        tile_out[e, 0] = first.astype(BF16)
        tile_out[e, 1] = last.astype(BF16)
        for side in range(2, 8):
            there, copy = halo_copy(e, side)
            pl.when(there)(copy.start)

    REACH = [(-1,), (-1, 0), (0, 1), (1,)]

    def conv(e, fields, held, matrix):
        def arrive(sides):
            for side in sides:
                dx, dz = SIDES[side]
                has_source, _ = near(-dx, -dz)
                _, copy = halo_copy(e, side)
                pl.when(has_source)(copy.wait_recv)

        def tile(side):
            return tile_in[e, side - 2].astype(F32)

        def spread(xp, field, low, high):
            wide = field.astype(F32)
            held[xp, ch : 2 * ch, :] = field
            for y in range(ny):
                part = block(wide, y)
                at = xp * 8 + y
                left = jnp.where(lane == 0, low[:, at : at + 1], pltpu.roll(part, 1, 1))
                right = jnp.where(
                    lane == LANES - 1, high[:, at : at + 1], pltpu.roll(part, LANES - 1, 1)
                )
                cols = slice(y * LANES, (y + 1) * LANES)
                held[xp, 0:ch, cols] = left.astype(BF16)
                held[xp, 2 * ch : 3 * ch, cols] = right.astype(BF16)

        def add(xp):
            steps = REACH[xp]
            low = 3 * ch * (steps[0] + 1)
            product = dot(matrix[low : low + 3 * ch * len(steps), :], held[xp])
            for n, ox in enumerate(steps):
                x = xp - 1 - ox
                for oy in (-1, 0, 1):
                    row = (3 * n + oy + 1) * ch
                    cols = slice((1 - oy) * LANES, (1 - oy) * LANES + width)
                    acc[x, :, cols] += product[row : row + ch]

        acc[...] = jnp.zeros(acc.shape, F32)
        arrive((3, 6))
        low, high = tile(3), tile(6)
        for xp in (1, 2):
            spread(xp, fields[xp - 1], low, high)
            add(xp)
        arrive((0, 1, 2, 4, 5, 7))
        spread(0, plane_in[e, 0], tile(4), tile(7))
        add(0)
        spread(3, plane_in[e, 1], tile(2), tile(5))
        add(3)
        return [acc[x, :, LANES : LANES + width] for x in range(2)]

    def tap_sums(deltas, held):
        for x in range(2):
            dpad[x, :, LANES : LANES + width] = deltas[x]
        total = [jnp.zeros((3 * ch, 3 * ch), F32) for _ in range(3)]
        for xp in range(4):
            steps = REACH[xp]
            rows = [
                dpad[xp - 1 - ox, :, (1 - oy) * LANES : (1 - oy) * LANES + width]
                for ox in steps
                for oy in (-1, 0, 1)
            ]
            product = dot_nt(jnp.concatenate(rows, axis=0), held[xp])
            for n, ox in enumerate(steps):
                total[ox + 1] = total[ox + 1] + product[3 * ch * n : 3 * ch * (n + 1)]
        return [total[i // 3][(i % 3) * ch : (i % 3 + 1) * ch] for i in range(9)]

    def pack_taps(taps, pack):
        for i in range(9):
            pack[i * ch : (i + 1) * ch, :] = taps[i][:, :LANES]
        for i in range(5):
            second = taps[2 * i + 1][:, LANES:] if i < 4 else jnp.zeros((ch, ch), F32)
            row = (9 + i) * ch
            pack[row : row + ch, :] = jnp.concatenate([taps[2 * i][:, LANES:], second], axis=1)

    class Reduce:
        def __init__(self, pack, wire, in_gz, part, mid, in_xy, full, sems):
            self.pack, self.wire, self.in_gz, self.part = pack, wire, in_gz, part
            self.mid, self.in_xy, self.full, self.sems = mid, in_xy, full, sems
            self.rows = pack.shape[0] // n_gz
            self.sub = self.rows // n_xy

        def copies(self, phase):
            result = []
            for k in range(1, n_gz if phase in (0, 3) else n_xy):
                if phase in (0, 3):
                    to = lax.rem(gz + k, n_gz)
                    target = (to, xy)
                else:
                    to = lax.rem(xy + k, n_xy)
                    target = (gz, to)
                source, landed = [
                    lambda: (self.wire.at[to], self.in_gz.at[k - 1]),
                    lambda: (self.mid.at[to], self.in_xy.at[k - 1]),
                    lambda: (self.full.at[gz, xy], self.full.at[gz, xy]),
                    lambda: (self.full.at[gz], self.full.at[gz]),
                ][phase]()
                result.append(
                    pltpu.make_async_remote_copy(
                        src_ref=source,
                        dst_ref=landed,
                        send_sem=self.sems.at[0, phase, k - 1],
                        recv_sem=self.sems.at[1, phase, k - 1],
                        device_id=target,
                        device_id_type=MESH,
                    )
                )
            return result

        def start(self, phase):
            for copy in self.copies(phase):
                copy.start()

        def finish(self, phase):
            for copy in self.copies(phase):
                copy.wait()

        def begin(self):
            for g in range(n_gz):
                self.wire[g] = self.pack[g * self.rows : (g + 1) * self.rows].astype(BF16)
            self.start(0)

        def second(self):
            self.finish(0)
            total = self.pack[pl.ds(pl.multiple_of(gz * self.rows, 16), self.rows), :]
            for k in range(n_gz - 1):
                total = total + self.in_gz[k].astype(F32)
            for j in range(n_xy):
                piece = total[j * self.sub : (j + 1) * self.sub]
                self.part[j] = piece
                self.mid[j] = piece.astype(BF16)
            self.start(1)

        def third(self):
            self.finish(1)
            total = self.part[xy]
            for k in range(n_xy - 1):
                total = total + self.in_xy[k].astype(F32)
            self.full[gz, xy] = total.astype(BF16)
            self.start(2)

        def fourth(self):
            self.finish(2)
            self.start(3)

        def done(self):
            self.finish(3)
            return self.full[...].reshape(self.rows * n_gz, LANES)

    sum_a = Reduce(pack_a, wire_a, in_a, part_a, mid_a, inx_a, full_a, sem_ra)
    sum_b = Reduce(pack_b, wire_b, in_b, part_b, mid_b, inx_b, full_b, sem_rb)

    lifted = []
    for a in range(2):
        pieces = []
        for y in range(ny):
            j, b = y // 2, y % 2
            row = (2 * a + b) * ch
            pieces.append(up[row : row + ch, j * LANES : (j + 1) * LANES])
        lifted.append((jnp.concatenate(pieces, axis=1) * plane_mask(a)).astype(BF16))
    send_halo(0, lifted)
    first = conv(0, lifted, s_lift, a1)
    acts = []
    for x in range(2):
        pre1[x] = first[x]
        acts.append((plane_mask(x) * first[x] * jax.nn.sigmoid(first[x])).astype(BF16))
    send_halo(1, acts)
    second = conv(1, acts, s_act, a2)
    deltas = []
    for x in range(2):
        v = second[x]
        sig = jax.nn.sigmoid(v)
        m = plane_mask(x)
        dec[:, x * width : (x + 1) * width] = (m * (v * sig)).astype(BF16)
        slope = sig * (1.0 + v * (1.0 - sig))
        deltas.append((cot_plane(x) * m * slope).astype(BF16))

    send_halo(2, deltas)
    taps_two = tap_sums(deltas, s_act)
    pack_taps(taps_two, pack_a)
    used = 14 * ch
    pack_a[used:, :] = jnp.zeros((pack_a.shape[0] - used, LANES), F32)
    sum_a.begin()
    back = conv(2, deltas, s_grad, b2)
    deltas = []
    for x in range(2):
        v = pre1[x]
        sig = jax.nn.sigmoid(v)
        slope = sig * (1.0 + v * (1.0 - sig))
        deltas.append((back[x] * plane_mask(x) * slope).astype(BF16))
    send_halo(3, deltas)
    pack_taps(tap_sums(deltas, s_lift), pack_b)
    sum_a.second()
    back = conv(3, deltas, s_grad, b1)
    du = [(back[x] * plane_mask(x)).astype(BF16) for x in range(2)]
    stacked = jnp.concatenate(
        [
            jnp.concatenate([block(du[a], 2 * j + b) for j in range(ny // 2)], axis=1)
            for a in range(2)
            for b in range(2)
        ],
        axis=0,
    )
    pack_b[used : used + 4 * ch, :] = dot_nt(stacked, parents)
    rest = used + 4 * ch
    if pack_b.shape[0] > rest:
        pack_b[rest:, :] = jnp.zeros((pack_b.shape[0] - rest, LANES), F32)
    sum_b.begin()
    by_parity = dot_tn(wup[...], stacked)
    kept = jnp.where(even, by_parity[:ch], by_parity[ch:])
    paired = kept + pltpu.roll(kept, half - 1, 1)
    parent_grad = jnp.where(even, paired, jnp.zeros_like(paired)).astype(BF16)
    wide_grad = jnp.concatenate([parent_grad, jnp.zeros_like(parent_grad)], axis=0)
    slot_grad[...] = dot_nt(hot, wide_grad).astype(BF16).reshape(slot_grad.shape)
    each_device(lambda k: back_copy(k).start())
    ret[me] = slot_grad[0]
    sum_a.third()
    sum_b.second()
    sum_a.fourth()
    sum_b.third()
    each_device(lambda k: back_copy(k).wait())
    returned = ret[...].reshape(slots, LANES).astype(F32).T[:ch]
    ret_out[...] = jnp.where(live, returned, 0.0).astype(BF16)
    out_a[...] = sum_a.done()
    sum_b.fourth()
    out_b[...] = sum_b.done()
    for e in range(4):
        for side in range(8):
            there, copy = halo_copy(e, side)
            pl.when(there)(copy.wait_send)


def finish_kernel(scale, dims, dec, ret, full_a, full_b, dec_out, ret_out, g1_out, g2_out, gup_out):
    ch, ny = dims
    width = ny * LANES
    for x in range(2):
        plane = dec[:, x * width : (x + 1) * width].astype(F32)
        dec_out[:, x] = plane.reshape(ch, ny, LANES).astype(BF16)
    ret_out[0] = ret[...]
    for full, out in ((full_b, g1_out), (full_a, g2_out)):
        for i in range(9):
            tile = full[i * ch : (i + 1) * ch].astype(F32) * scale
            out[3 * i] = tile[:, :ch]
            out[3 * i + 1] = tile[:, ch:]
            pair = full[(9 + i // 2) * ch : (10 + i // 2) * ch].astype(F32) * scale
            out[3 * i + 2] = pair[:, :ch] if i % 2 == 0 else pair[:, ch:]
    for p in range(4):
        tile = full_b[(14 + p) * ch : (15 + p) * ch].astype(F32) * scale
        gup_out[2 * p] = tile[:, :ch]
        gup_out[2 * p + 1] = tile[:, ch:]


def local(
    parent_feat, parent_cell, send_count, up_weight, conv_one, conv_two, child_mask, cotangent
):
    ch, size_x, ny, size_z = cotangent.shape
    n_gz, n_xy = lax.axis_size("gz"), lax.axis_size("xy")
    n_dev = n_gz * n_xy
    slot_total = parent_feat.shape[2]
    cap = slot_total // n_dev
    voxels = size_x * ny * size_z
    width = ny * size_z
    unit = n_dev * 16
    rows_a = -(-14 * ch // unit) * unit
    rows_b = -(-18 * ch // unit) * unit

    def reduce_scratch(rows):
        per = rows // n_gz
        sub = per // n_xy
        return [
            pltpu.VMEM((rows, LANES), F32),
            pltpu.VMEM((n_gz, per, LANES), BF16),
            pltpu.VMEM((n_gz - 1, per, LANES), BF16),
            pltpu.VMEM((n_xy, sub, LANES), F32),
            pltpu.VMEM((n_xy, sub, LANES), BF16),
            pltpu.VMEM((n_xy - 1, sub, LANES), BF16),
            pltpu.VMEM((n_gz, n_xy, sub, LANES), BF16),
        ]

    vmem = pl.BlockSpec(memory_space=pltpu.VMEM)
    most = max(n_gz, n_xy) - 1
    dma = pltpu.SemaphoreType.DMA
    dec, ret, full_a, full_b = pl.pallas_call(
        functools.partial(all_kernel, (n_gz, n_xy, ch, ny)),
        out_shape=(
            jax.ShapeDtypeStruct((ch, voxels), BF16),
            jax.ShapeDtypeStruct((ch, slot_total), BF16),
            jax.ShapeDtypeStruct((rows_a, LANES), BF16),
            jax.ShapeDtypeStruct((rows_b, LANES), BF16),
        ),
        in_specs=[vmem] * 8,
        out_specs=(vmem,) * 4,
        scratch_shapes=[
            pltpu.VMEM((n_dev, cap, LANES), BF16),
            pltpu.VMEM((4 * ch, 2 * ch), BF16),
            pltpu.VMEM((n_dev, cap, LANES), BF16),
            pltpu.VMEM((n_dev, cap, LANES), BF16),
            pltpu.VMEM((n_dev, cap, LANES), BF16),
            pltpu.VMEM((9 * ch, 3 * ch), BF16),
            pltpu.VMEM((9 * ch, 3 * ch), BF16),
            pltpu.VMEM((9 * ch, 3 * ch), BF16),
            pltpu.VMEM((9 * ch, 3 * ch), BF16),
            pltpu.VMEM((4, 2, ch, width), BF16),
            pltpu.VMEM((4, 2, ch, width), BF16),
            pltpu.VMEM((4, 2, ch, LANES), BF16),
            pltpu.VMEM((4, 6, ch, LANES), BF16),
            pltpu.VMEM((4, 3 * ch, width), BF16),
            pltpu.VMEM((4, 3 * ch, width), BF16),
            pltpu.VMEM((4, 3 * ch, width), BF16),
            pltpu.VMEM((2, ch, width + 2 * LANES), F32),
            pltpu.VMEM((2, ch, width + 2 * LANES), BF16),
            pltpu.VMEM((2, ch, width), F32),
            *reduce_scratch(rows_a),
            *reduce_scratch(rows_b),
            dma((2, n_dev)),
            dma((2, n_dev)),
            dma((2, 4, 8)),
            dma((2, 4, most)),
            dma((2, 4, most)),
        ],
        compiler_params=pltpu.CompilerParams(
            collective_id=0, has_side_effects=True, vmem_limit_bytes=56 * 1024 * 1024
        ),
    )(parent_feat, parent_cell, send_count, up_weight, conv_one, conv_two, child_mask, cotangent)
    scale = 1.0 / math.sqrt(size_x * n_xy * ny * size_z * n_gz)
    return pl.pallas_call(
        functools.partial(finish_kernel, scale, (ch, ny)),
        out_shape=(
            jax.ShapeDtypeStruct(cotangent.shape, BF16),
            jax.ShapeDtypeStruct((1, ch, slot_total), BF16),
            jax.ShapeDtypeStruct((27, ch, ch), F32),
            jax.ShapeDtypeStruct((27, ch, ch), F32),
            jax.ShapeDtypeStruct((8, ch, ch), F32),
        ),
        in_specs=[vmem] * 4,
        out_specs=(vmem,) * 5,
    )(dec, ret, full_a, full_b)


def solution(mesh):
    placed = (
        P(("gz", "xy"), None, None),
        P(("gz", "xy"), None),
        P(("gz", "xy"), None),
        P(),
        P(),
        P(),
        P("xy", None, "gz"),
        P(None, "xy", None, "gz"),
    )
    return jax.shard_map(
        local,
        mesh=mesh,
        in_specs=placed,
        out_specs=(P(None, "xy", None, "gz"), P(("gz", "xy"), None, None), P(), P(), P()),
        check_vma=False,
    )
```

```python
import functools
import math

import jax
import jax.numpy as jnp
from jax import lax
from jax.experimental import pallas as pl
from jax.experimental.pallas import tpu as pltpu
from jax.sharding import PartitionSpec as P

MESH = pl.DeviceIdType.MESH
F32 = jnp.float32
BF16 = jnp.bfloat16
LANES = 128
USED = [range(8), (3, 6), range(8), range(8), (0, 1)]
SIDES = [(1, 0), (-1, 0), (-1, 1), (0, 1), (1, 1), (-1, -1), (0, -1), (1, -1)]


def dot(a, b):
    return jnp.dot(a, b, preferred_element_type=F32)


def dot_nt(a, b):
    return lax.dot_general(a, b, (((1,), (1,)), ((), ())), preferred_element_type=F32)


def dot_tn(a, b):
    return lax.dot_general(a, b, (((0,), (0,)), ((), ())), preferred_element_type=F32)


def all_kernel(
    dims,
    feat, cell, count, w_up, w1, w2, mask_in, cot_in,
    dec, ret_out, out_a, out_b, out_c,
    src, wup, got, slot_grad, ret,
    a1, b1, a2, b2,
    grid, grid_in, mask_out, mask_halo,
    planes, plane_in, tile_out, tile_in,
    s_lift, s_act, s_grad, acc, dpad, pre1,
    pack_a, wire_a, in_a, part_a, mid_a, inx_a, full_a,
    pack_b, wire_b, in_b, part_b, mid_b, inx_b, full_b,
    pack_c, in_c, full_c,
    sem_to, sem_back, sem_halo, sem_ra, sem_rb, sem_c,
):
    n_gz, n_xy, ch, ny = dims
    n_dev = n_gz * n_xy
    width = ny * LANES
    gz = lax.axis_index("gz")
    xy = lax.axis_index("xy")
    me = gz * n_xy + xy

    barrier = pltpu.get_barrier_semaphore()

    def greet(k, carry):
        to = lax.rem(me + k, n_dev)
        pl.semaphore_signal(
            barrier, inc=1, device_id=(to // n_xy, lax.rem(to, n_xy)), device_id_type=MESH
        )
        return carry

    lax.fori_loop(1, n_dev, greet, 0)

    def weights(i, carry):
        rows = pl.ds(pl.multiple_of(i * ch, ch), ch)
        for w, a, b in ((w1, a1, b1), (w2, a2, b2)):
            a[rows, :] = jnp.concatenate([w[3 * i + t] for t in range(3)], axis=1)
            b[rows, :] = jnp.concatenate(
                [w[26 - 3 * i - t].astype(F32).T.astype(BF16) for t in range(3)], axis=1
            )
        return carry

    def near(dx, dz):
        x, z = xy + dx, gz + dz
        there = (x >= 0) & (x < n_xy) & (z >= 0) & (z < n_gz)
        return there, (z, x)

    def landing(e, side):
        dx, dz = SIDES[side]
        if dz != 0:
            return tile_in.at[e, side - 2]
        return {0: grid_in, 4: mask_halo}[e].at[side] if e in (0, 4) else plane_in.at[e - 2, side]

    def halo_copy(e, side):
        dx, dz = SIDES[side]
        there, target = near(dx, dz)
        if e == 0 and dz == 0:
            source = grid
        elif e == 4:
            source = mask_out
        elif dz == 0:
            source = planes.at[e - 2, 1 if dx > 0 else 0]
        else:
            source = tile_out.at[e, 1 if dz > 0 else 0]
        return there, pltpu.make_async_remote_copy(
            src_ref=source,
            dst_ref=landing(e, side),
            send_sem=sem_halo.at[0, e, side],
            recv_sem=sem_halo.at[1, e, side],
            device_id=target,
            device_id_type=MESH,
        )

    for side, (dx, dz) in enumerate(SIDES):
        has_source, _ = near(-dx, -dz)

        @pl.when(jnp.logical_not(has_source))
        def _():
            for e in [e for e in range(5) if side in USED[e]]:
                ref = landing(e, side)
                ref[...] = jnp.zeros(ref.shape, BF16)

    dpad[...] = jnp.zeros(dpad.shape, BF16)
    slots = got.shape[0] * got.shape[1]
    cap = got.shape[1]
    slot = lax.broadcasted_iota(jnp.int32, (1, slots), 1)
    to_slot = lax.broadcasted_iota(jnp.int32, (n_dev, slots), 0) == slot // cap
    counts = jnp.broadcast_to(count[...].astype(F32), (8, n_dev)).astype(BF16)
    counts = dot(counts, jnp.where(to_slot, 1.0, 0.0).astype(BF16))[:1]
    live = lax.rem(slot, cap).astype(F32) < counts
    sent = jnp.concatenate(
        [
            jnp.where(live, feat[0].astype(F32), 0.0),
            jnp.broadcast_to(cell[...].astype(F32), (8, slots)),
            jnp.zeros((LANES - ch - 8, slots), F32),
        ],
        axis=0,
    )
    src[...] = sent.T.astype(BF16).reshape(src.shape)
    for i in range(4):
        wup[i * ch : (i + 1) * ch, :] = jnp.concatenate([w_up[2 * i], w_up[2 * i + 1]], axis=1)
    mask_out[...] = jnp.concatenate([mask_in[0], mask_in[1]], axis=0).astype(F32).astype(BF16)
    pl.semaphore_wait(barrier, n_dev - 1)

    def to_copy(k):
        to = lax.rem(me + k, n_dev)
        return pltpu.make_async_remote_copy(
            src_ref=src.at[to],
            dst_ref=got.at[k],
            send_sem=sem_to.at[0, k],
            recv_sem=sem_to.at[1, k],
            device_id=(to // n_xy, lax.rem(to, n_xy)),
            device_id_type=MESH,
        )

    def back_copy(k):
        to = lax.rem(me + n_dev - k, n_dev)
        return pltpu.make_async_remote_copy(
            src_ref=slot_grad.at[k],
            dst_ref=ret.at[me],
            send_sem=sem_back.at[0, k],
            recv_sem=sem_back.at[1, k],
            device_id=(to // n_xy, lax.rem(to, n_xy)),
            device_id_type=MESH,
        )

    def each_device(action):
        def step(k, carry):
            action(k)
            return carry

        lax.fori_loop(1, n_dev, step, 0)

    each_device(lambda k: to_copy(k).start())
    for side in USED[4]:
        there, copy = halo_copy(4, side)
        pl.when(there)(copy.start)
    got[0] = src[me]
    lax.fori_loop(0, 9, weights, 0)
    each_device(lambda k: to_copy(k).wait())

    listed = got[...].reshape(slots, LANES)
    half = 4 * LANES
    cells = listed[:, ch : ch + 1].astype(F32)
    owner = lax.broadcasted_iota(jnp.int32, (1, half // 2), 1).astype(F32)
    hot = jnp.where(cells == owner, 1.0, 0.0).astype(BF16)
    grid[...] = dot_tn(listed, hot)[:ch].astype(BF16)
    for side in (0, 1):
        there, copy = halo_copy(0, side)
        pl.when(there)(copy.start)
    column = lax.broadcasted_iota(jnp.int32, (1, half), 1)
    even = lax.rem(column, 2) == 0
    twice = jnp.where(
        lax.broadcasted_iota(jnp.int32, (LANES, 2 * LANES), 0)
        == lax.broadcasted_iota(jnp.int32, (LANES, 2 * LANES), 1) // 2,
        1.0,
        0.0,
    ).astype(BF16)

    def by_parity_of(values):
        wide = jnp.concatenate([dot(values[:, :LANES], twice), dot(values[:, LANES:], twice)], axis=1)
        none = jnp.zeros_like(wide)
        return jnp.concatenate(
            [jnp.where(even, wide, none), jnp.where(even, none, wide)], axis=0
        ).astype(BF16)

    def mask_row(tile, x):
        return jnp.concatenate([tile[x * ny + y : x * ny + y + 1] for y in range(ny)], axis=1)

    def lift(listed_parents, tile):
        up = dot(wup[...], listed_parents)
        result = []
        for a in range(2):
            pieces = []
            for y in range(ny):
                row = (2 * a + y % 2) * ch
                pieces.append(up[row : row + ch, (y // 2) * LANES : (y // 2 + 1) * LANES])
            result.append((jnp.concatenate(pieces, axis=1) * mask_row(tile, a)).astype(BF16))
        return result

    parents = by_parity_of(grid[...])
    own_mask = mask_out[...].astype(F32)

    lane = lax.broadcasted_iota(jnp.int32, (1, LANES), 1)

    def block(value, y):
        return value[:, y * LANES : (y + 1) * LANES]

    def plane_mask(x):
        return mask_row(own_mask, x)

    def cot_plane(x):
        return cot_in[:, x].astype(F32).reshape(ch, width)

    def send_planes(e, fields):
        for x in range(2):
            planes[e - 2, x] = fields[x]
        for side in (0, 1):
            there, copy = halo_copy(e, side)
            pl.when(there)(copy.start)

    def send_edges(e, fields, shift):
        period = len(fields) * ny
        edge = lax.rem(lane, period)
        first = jnp.zeros((ch, LANES), F32)
        last = jnp.zeros((ch, LANES), F32)
        for x, field in enumerate(fields):
            wide = field.astype(F32)
            for y in range(ny):
                here = edge == (shift + x * ny + y) % period
                part = block(wide, y)
                first = jnp.where(here, part[:, :1], first)
                last = jnp.where(here, part[:, LANES - 1 :], last)
        tile_out[e, 0] = first.astype(BF16)
        tile_out[e, 1] = last.astype(BF16)
        for side in (3, 6, 2, 4, 5, 7):
            if side in USED[e]:
                there, copy = halo_copy(e, side)
                pl.when(there)(copy.start)

    def arrive(e, sides):
        for side in sides:
            dx, dz = SIDES[side]
            has_source, _ = near(-dx, -dz)
            _, copy = halo_copy(e, side)
            pl.when(has_source)(copy.wait_recv)

    def tile(e, side):
        return tile_in[e, side - 2].astype(F32)

    def spread(held, xp, field, low, high):
        wide = field.astype(F32)
        held[xp, ch : 2 * ch, :] = field
        for y in range(ny):
            part = block(wide, y)
            at = xp * ny + y
            left = jnp.where(lane == 0, low[:, at : at + 1], pltpu.roll(part, 1, 1))
            right = jnp.where(
                lane == LANES - 1, high[:, at : at + 1], pltpu.roll(part, LANES - 1, 1)
            )
            cols = slice(y * LANES, (y + 1) * LANES)
            held[xp, 0:ch, cols] = left.astype(BF16)
            held[xp, 2 * ch : 3 * ch, cols] = right.astype(BF16)

    def reach(xp, count):
        return [ox for ox in (-1, 0, 1) if 0 <= xp - 1 - ox < count]

    def add(matrix, held, xp, count):
        steps = reach(xp, count)
        low = 3 * ch * (steps[0] + 1)
        product = dot(matrix[low : low + 3 * ch * len(steps), :], held[xp])
        for n, ox in enumerate(steps):
            x = xp - 1 - ox
            for oy in (-1, 0, 1):
                row = (3 * n + oy + 1) * ch
                cols = slice((1 - oy) * LANES, (1 - oy) * LANES + width)
                acc[x, :, cols] += product[row : row + ch]

    def result(count):
        return [acc[x, :, LANES : LANES + width] for x in range(count)]

    def conv(e, fields, held, matrix):
        acc[...] = jnp.zeros(acc.shape, F32)
        arrive(e, (3, 6))
        low, high = tile(e, 3), tile(e, 6)
        for xp in (1, 2):
            spread(held, xp, fields[xp - 1], low, high)
            add(matrix, held, xp, 2)
        arrive(e, (0, 1, 2, 4, 5, 7))
        spread(held, 0, plane_in[e - 2, 0], tile(e, 4), tile(e, 7))
        add(matrix, held, 0, 2)
        spread(held, 3, plane_in[e - 2, 1], tile(e, 2), tile(e, 5))
        add(matrix, held, 3, 2)
        return result(2)

    def tap_sums(deltas, held, start):
        for x in range(2):
            dpad[x, :, LANES : LANES + width] = deltas[x]
        total = [jnp.zeros((3 * ch, 3 * ch), F32) for _ in range(3)]
        for xp in range(4):
            steps = reach(xp, 2)
            rows = [
                dpad[xp - 1 - ox, :, (1 - oy) * LANES : (1 - oy) * LANES + width]
                for ox in steps
                for oy in (-1, 0, 1)
            ]
            product = dot_nt(jnp.concatenate(rows, axis=0), held[start + xp])
            for n, ox in enumerate(steps):
                total[ox + 1] = total[ox + 1] + product[3 * ch * n : 3 * ch * (n + 1)]
        return [total[i // 3][(i % 3) * ch : (i % 3 + 1) * ch] for i in range(9)]

    def pack_taps(taps, pack):
        for i in range(9):
            pack[i * ch : (i + 1) * ch, :] = taps[i][:, :LANES]
        for i in range(5):
            second = taps[2 * i + 1][:, LANES:] if i < 4 else jnp.zeros((ch, ch), F32)
            row = (9 + i) * ch
            pack[row : row + ch, :] = jnp.concatenate([taps[2 * i][:, LANES:], second], axis=1)

    class Reduce:
        def __init__(self, pack, wire, in_gz, part, mid, in_xy, full, sems):
            self.pack, self.wire, self.in_gz, self.part = pack, wire, in_gz, part
            self.mid, self.in_xy, self.full, self.sems = mid, in_xy, full, sems
            self.rows = pack.shape[0] // n_gz
            self.sub = self.rows // n_xy

        def copies(self, phase):
            result = []
            for k in range(1, n_gz if phase in (0, 3) else n_xy):
                if phase in (0, 3):
                    to = lax.rem(gz + k, n_gz)
                    target = (to, xy)
                else:
                    to = lax.rem(xy + k, n_xy)
                    target = (gz, to)
                source, landed = [
                    lambda: (self.wire.at[to], self.in_gz.at[k - 1]),
                    lambda: (self.mid.at[to], self.in_xy.at[k - 1]),
                    lambda: (self.full.at[gz, xy], self.full.at[gz, xy]),
                    lambda: (self.full.at[gz], self.full.at[gz]),
                ][phase]()
                result.append(
                    pltpu.make_async_remote_copy(
                        src_ref=source,
                        dst_ref=landed,
                        send_sem=self.sems.at[0, phase, k - 1],
                        recv_sem=self.sems.at[1, phase, k - 1],
                        device_id=target,
                        device_id_type=MESH,
                    )
                )
            return result

        def start(self, phase):
            for copy in self.copies(phase):
                copy.start()

        def finish(self, phase):
            for copy in self.copies(phase):
                copy.wait()

        def begin(self):
            for g in range(n_gz):
                self.wire[g] = self.pack[g * self.rows : (g + 1) * self.rows].astype(BF16)
            self.start(0)

        def second(self):
            self.finish(0)
            total = self.pack[pl.ds(pl.multiple_of(gz * self.rows, 16), self.rows), :]
            for k in range(n_gz - 1):
                total = total + self.in_gz[k].astype(F32)
            for j in range(n_xy):
                piece = total[j * self.sub : (j + 1) * self.sub]
                self.part[j] = piece
                self.mid[j] = piece.astype(BF16)
            self.start(1)

        def third(self):
            self.finish(1)
            total = self.part[xy]
            for k in range(n_xy - 1):
                total = total + self.in_xy[k].astype(F32)
            self.full[gz, xy] = total.astype(BF16)
            self.start(2)

        def fourth(self):
            self.finish(2)
            self.start(3)

        def done(self):
            self.finish(3)
            return self.full[...].reshape(self.rows * n_gz, LANES)

    sum_a = Reduce(pack_a, wire_a, in_a, part_a, mid_a, inx_a, full_a, sem_ra)
    sum_b = Reduce(pack_b, wire_b, in_b, part_b, mid_b, inx_b, full_b, sem_rb)

    lifted = lift(parents, own_mask)
    send_edges(0, lifted, 0)
    acc[...] = jnp.zeros(acc.shape, F32)
    arrive(0, (3, 6))
    low, high = tile(0, 3), tile(0, 6)
    for x in range(2):
        spread(s_lift, x + 2, lifted[x], low, high)
        add(a1, s_lift, x + 2, 4)
    arrive(4, (0, 1))
    arrive(0, (0, 1, 2, 4, 5, 7))
    around = []
    for side in (0, 1):
        around.append(mask_halo[side].astype(F32))
        beside = lift(by_parity_of(grid_in[side]), around[side])
        low, high = (tile(0, 4), tile(0, 7)) if side == 0 else (tile(0, 2), tile(0, 5))
        for x in range(2):
            xp = 4 * side + x
            spread(s_lift, xp, beside[x], low, high)
            add(a1, s_lift, xp, 4)
    first = result(4)
    rows = [mask_row(around[0], 1), plane_mask(0), plane_mask(1), mask_row(around[1], 0)]
    acts = [(rows[x] * first[x] * jax.nn.sigmoid(first[x])).astype(BF16) for x in range(4)]
    send_edges(1, acts, 0)
    for x in range(2):
        pre1[x] = first[x + 1]
    acc[...] = jnp.zeros(acc.shape, F32)
    arrive(1, (3, 6))
    low, high = tile(1, 3), tile(1, 6)
    for xp in range(4):
        spread(s_act, xp, acts[xp], low, high)
        add(a2, s_act, xp, 2)
    second = result(2)
    deltas = []
    for x in range(2):
        v = second[x]
        sig = jax.nn.sigmoid(v)
        m = plane_mask(x)
        dec[:, x * width : (x + 1) * width] = (m * (v * sig)).astype(BF16)
        slope = sig * (1.0 + v * (1.0 - sig))
        deltas.append((cot_plane(x) * m * slope).astype(BF16))

    used = 14 * ch
    for pack in (pack_a, pack_b):
        if pack.shape[0] > used:
            pack[used:, :] = jnp.zeros((pack.shape[0] - used, LANES), F32)
    send_planes(2, deltas)
    send_edges(2, deltas, 8)
    pack_taps(tap_sums(deltas, s_act, 0), pack_a)
    sum_a.begin()
    back = conv(2, deltas, s_grad, b2)
    deltas = []
    for x in range(2):
        v = pre1[x]
        sig = jax.nn.sigmoid(v)
        slope = sig * (1.0 + v * (1.0 - sig))
        deltas.append((back[x] * plane_mask(x) * slope).astype(BF16))
    send_planes(3, deltas)
    send_edges(3, deltas, 8)
    pack_taps(tap_sums(deltas, s_lift, 1), pack_b)
    sum_b.begin()
    sum_a.second()
    back = conv(3, deltas, s_grad, b1)
    sum_b.second()
    sum_a.third()
    du = [(back[x] * plane_mask(x)).astype(BF16) for x in range(2)]
    stacked = jnp.concatenate(
        [
            jnp.concatenate([block(du[a], 2 * j + b) for j in range(ny // 2)], axis=1)
            for a in range(2)
            for b in range(2)
        ],
        axis=0,
    )
    grad_up = dot_nt(stacked, parents)
    part_c = pack_c.shape[1]
    for d in range(pack_c.shape[0]):
        if (d + 1) * part_c <= 4 * ch:
            pack_c[d] = grad_up[d * part_c : (d + 1) * part_c]
        else:
            pack_c[d] = jnp.zeros((part_c, LANES), F32)

    def scatter_copy(k):
        to = lax.rem(me + k, n_dev)
        return pltpu.make_async_remote_copy(
            src_ref=pack_c.at[to],
            dst_ref=in_c.at[k],
            send_sem=sem_c.at[0, 0, k],
            recv_sem=sem_c.at[0, 1, k],
            device_id=(to // n_xy, lax.rem(to, n_xy)),
            device_id_type=MESH,
        )

    def gather_copy(k):
        to = lax.rem(me + k, n_dev)
        return pltpu.make_async_remote_copy(
            src_ref=full_c.at[me],
            dst_ref=full_c.at[me],
            send_sem=sem_c.at[1, 0, k],
            recv_sem=sem_c.at[1, 1, k],
            device_id=(to // n_xy, lax.rem(to, n_xy)),
            device_id_type=MESH,
        )

    each_device(lambda k: scatter_copy(k).start())
    in_c[0] = pack_c[me]
    by_parity = dot_tn(wup[...], stacked)
    kept = jnp.where(even, by_parity[:ch], by_parity[ch:])
    paired = kept + pltpu.roll(kept, half - 1, 1)
    parent_grad = jnp.where(even, paired, jnp.zeros_like(paired)).astype(BF16)
    compact = jnp.concatenate(
        [dot_nt(parent_grad[:, h * 2 * LANES : (h + 1) * 2 * LANES], twice) for h in range(2)],
        axis=1,
    )
    compact = jnp.concatenate([compact, jnp.zeros_like(compact)], axis=0).astype(BF16)
    slot_grad[...] = dot_nt(hot, compact).astype(BF16).reshape(slot_grad.shape)
    each_device(lambda k: back_copy(k).start())
    ret[me] = slot_grad[0]
    sum_b.third()
    sum_a.fourth()
    each_device(lambda k: scatter_copy(k).wait())
    total = in_c[0]
    for d in range(1, n_dev):
        total = total + in_c[d]
    full_c[me] = total
    each_device(lambda k: gather_copy(k).start())
    sum_b.fourth()
    each_device(lambda k: back_copy(k).wait())
    returned = ret[...].reshape(slots, LANES).astype(F32).T[:ch]
    ret_out[...] = jnp.where(live, returned, 0.0).astype(BF16)
    out_a[...] = sum_a.done()
    each_device(lambda k: gather_copy(k).wait())
    out_c[...] = full_c[...].reshape(out_c.shape)
    out_b[...] = sum_b.done()
    for e in range(5):
        for side in USED[e]:
            there, copy = halo_copy(e, side)
            pl.when(there)(copy.wait_send)


def finish_kernel(scale, dims, dec, ret, full_a, full_b, full_c, dec_out, ret_out, g1_out, g2_out, gup_out):
    ch, ny = dims
    width = ny * LANES
    for x in range(2):
        plane = dec[:, x * width : (x + 1) * width].astype(F32)
        dec_out[:, x] = plane.reshape(ch, ny, LANES).astype(BF16)
    ret_out[0] = ret[...]
    for full, out in ((full_b, g1_out), (full_a, g2_out)):
        for i in range(9):
            tile = full[i * ch : (i + 1) * ch].astype(F32) * scale
            out[3 * i] = tile[:, :ch]
            out[3 * i + 1] = tile[:, ch:]
            pair = full[(9 + i // 2) * ch : (10 + i // 2) * ch].astype(F32) * scale
            out[3 * i + 2] = pair[:, :ch] if i % 2 == 0 else pair[:, ch:]
    for p in range(4):
        tile = full_c[p * ch : (p + 1) * ch] * scale
        gup_out[2 * p] = tile[:, :ch]
        gup_out[2 * p + 1] = tile[:, ch:]


def local(
    parent_feat, parent_cell, send_count, up_weight, conv_one, conv_two, child_mask, cotangent
):
    ch, size_x, ny, size_z = cotangent.shape
    n_gz, n_xy = lax.axis_size("gz"), lax.axis_size("xy")
    n_dev = n_gz * n_xy
    slot_total = parent_feat.shape[2]
    cap = slot_total // n_dev
    voxels = size_x * ny * size_z
    width = ny * size_z
    unit = n_dev * 16
    rows_a = -(-14 * ch // unit) * unit
    rows_c = -(-4 * ch // (8 * n_dev)) * 8 * n_dev

    def reduce_scratch(rows):
        per = rows // n_gz
        sub = per // n_xy
        return [
            pltpu.VMEM((rows, LANES), F32),
            pltpu.VMEM((n_gz, per, LANES), BF16),
            pltpu.VMEM((n_gz - 1, per, LANES), BF16),
            pltpu.VMEM((n_xy, sub, LANES), F32),
            pltpu.VMEM((n_xy, sub, LANES), BF16),
            pltpu.VMEM((n_xy - 1, sub, LANES), BF16),
            pltpu.VMEM((n_gz, n_xy, sub, LANES), BF16),
        ]

    vmem = pl.BlockSpec(memory_space=pltpu.VMEM)
    most = max(n_gz, n_xy) - 1
    dma = pltpu.SemaphoreType.DMA
    dec, ret, full_a, full_b, full_c = pl.pallas_call(
        functools.partial(all_kernel, (n_gz, n_xy, ch, ny)),
        out_shape=(
            jax.ShapeDtypeStruct((ch, voxels), BF16),
            jax.ShapeDtypeStruct((ch, slot_total), BF16),
            jax.ShapeDtypeStruct((rows_a, LANES), BF16),
            jax.ShapeDtypeStruct((rows_a, LANES), BF16),
            jax.ShapeDtypeStruct((rows_c, LANES), F32),
        ),
        in_specs=[vmem] * 8,
        out_specs=(vmem,) * 5,
        scratch_shapes=[
            pltpu.VMEM((n_dev, cap, LANES), BF16),
            pltpu.VMEM((4 * ch, 2 * ch), BF16),
            pltpu.VMEM((n_dev, cap, LANES), BF16),
            pltpu.VMEM((n_dev, cap, LANES), BF16),
            pltpu.VMEM((n_dev, cap, LANES), BF16),
            pltpu.VMEM((9 * ch, 3 * ch), BF16),
            pltpu.VMEM((9 * ch, 3 * ch), BF16),
            pltpu.VMEM((9 * ch, 3 * ch), BF16),
            pltpu.VMEM((9 * ch, 3 * ch), BF16),
            pltpu.VMEM((ch, 2 * LANES), BF16),
            pltpu.VMEM((2, ch, 2 * LANES), BF16),
            pltpu.VMEM((2 * ny, LANES), BF16),
            pltpu.VMEM((2, 2 * ny, LANES), BF16),
            pltpu.VMEM((2, 2, ch, width), BF16),
            pltpu.VMEM((2, 2, ch, width), BF16),
            pltpu.VMEM((4, 2, ch, LANES), BF16),
            pltpu.VMEM((4, 6, ch, LANES), BF16),
            pltpu.VMEM((6, 3 * ch, width), BF16),
            pltpu.VMEM((4, 3 * ch, width), BF16),
            pltpu.VMEM((4, 3 * ch, width), BF16),
            pltpu.VMEM((4, ch, width + 2 * LANES), F32),
            pltpu.VMEM((2, ch, width + 2 * LANES), BF16),
            pltpu.VMEM((2, ch, width), F32),
            *reduce_scratch(rows_a),
            *reduce_scratch(rows_a),
            pltpu.VMEM((n_dev, rows_c // n_dev, LANES), F32),
            pltpu.VMEM((n_dev, rows_c // n_dev, LANES), F32),
            pltpu.VMEM((n_dev, rows_c // n_dev, LANES), F32),
            dma((2, n_dev)),
            dma((2, n_dev)),
            dma((2, 5, 8)),
            dma((2, 4, most)),
            dma((2, 4, most)),
            dma((2, 2, n_dev)),
        ],
        compiler_params=pltpu.CompilerParams(
            collective_id=0, has_side_effects=True, vmem_limit_bytes=56 * 1024 * 1024
        ),
    )(parent_feat, parent_cell, send_count, up_weight, conv_one, conv_two, child_mask, cotangent)
    scale = 1.0 / math.sqrt(size_x * n_xy * ny * size_z * n_gz)
    return pl.pallas_call(
        functools.partial(finish_kernel, scale, (ch, ny)),
        out_shape=(
            jax.ShapeDtypeStruct(cotangent.shape, BF16),
            jax.ShapeDtypeStruct((1, ch, slot_total), BF16),
            jax.ShapeDtypeStruct((27, ch, ch), F32),
            jax.ShapeDtypeStruct((27, ch, ch), F32),
            jax.ShapeDtypeStruct((8, ch, ch), F32),
        ),
        in_specs=[vmem] * 5,
        out_specs=(vmem,) * 5,
    )(dec, ret, full_a, full_b, full_c)


def solution(mesh):
    placed = (
        P(("gz", "xy"), None, None),
        P(("gz", "xy"), None),
        P(("gz", "xy"), None),
        P(),
        P(),
        P(),
        P("xy", None, "gz"),
        P(None, "xy", None, "gz"),
    )
    return jax.shard_map(
        local,
        mesh=mesh,
        in_specs=placed,
        out_specs=(P(None, "xy", None, "gz"), P(("gz", "xy"), None, None), P(), P(), P()),
        check_vma=False,
    )
```

```python
import functools
import math

import jax
import jax.numpy as jnp
from jax import lax
from jax.experimental import pallas as pl
from jax.experimental.pallas import tpu as pltpu
from jax.sharding import PartitionSpec as P

MESH = pl.DeviceIdType.MESH
F32 = jnp.float32
BF16 = jnp.bfloat16
LANES = 128
USED = [range(8), (3, 6), range(8), range(8), (0, 1)]
SIDES = [(1, 0), (-1, 0), (-1, 1), (0, 1), (1, 1), (-1, -1), (0, -1), (1, -1)]


def dot(a, b):
    return jnp.dot(a, b, preferred_element_type=F32)


def dot_nt(a, b):
    return lax.dot_general(a, b, (((1,), (1,)), ((), ())), preferred_element_type=F32)


def dot_tn(a, b):
    return lax.dot_general(a, b, (((0,), (0,)), ((), ())), preferred_element_type=F32)


def all_kernel(
    dims,
    feat, cell, count, w_up, w1, w2, mask_in, cot_in,
    dec, ret_out, out_a, out_b, out_c,
    src, wup, got, slot_grad, ret,
    a1, b1, a2, b2,
    grid, grid_in, mask_out, mask_halo,
    planes, plane_in, tile_out, tile_in,
    s_lift, s_act, s_grad, acc, dpad, pre1,
    pack_a, wire_a, in_a, part_a, mid_a, inx_a, full_a,
    pack_b, wire_b, in_b, part_b, mid_b, inx_b, full_b,
    full_c,
    sem_to, sem_back, sem_halo, sem_ra, sem_rb, sem_c,
):
    n_gz, n_xy, ch, ny = dims
    n_dev = n_gz * n_xy
    width = ny * LANES
    gz = lax.axis_index("gz")
    xy = lax.axis_index("xy")
    me = gz * n_xy + xy

    barrier = pltpu.get_barrier_semaphore()

    def greet(k, carry):
        to = lax.rem(me + k, n_dev)
        pl.semaphore_signal(
            barrier, inc=1, device_id=(to // n_xy, lax.rem(to, n_xy)), device_id_type=MESH
        )
        return carry

    lax.fori_loop(1, n_dev, greet, 0)

    def stack_forward(w, into):
        def step(i, carry):
            rows = pl.ds(pl.multiple_of(i * ch, ch), ch)
            into[rows, :] = jnp.concatenate([w[3 * i + t] for t in range(3)], axis=1)
            return carry

        lax.fori_loop(0, 9, step, 0)

    def stack_backward(w, into):
        def step(i, carry):
            rows = pl.ds(pl.multiple_of(i * ch, ch), ch)
            into[rows, :] = jnp.concatenate(
                [w[26 - 3 * i - t].astype(F32).T.astype(BF16) for t in range(3)], axis=1
            )
            return carry

        lax.fori_loop(0, 9, step, 0)

    def near(dx, dz):
        x, z = xy + dx, gz + dz
        there = (x >= 0) & (x < n_xy) & (z >= 0) & (z < n_gz)
        return there, (z, x)

    def landing(e, side):
        dx, dz = SIDES[side]
        if dz != 0:
            return tile_in.at[e, side - 2]
        return {0: grid_in, 4: mask_halo}[e].at[side] if e in (0, 4) else plane_in.at[e - 2, side]

    def halo_copy(e, side):
        dx, dz = SIDES[side]
        there, target = near(dx, dz)
        if e == 0 and dz == 0:
            source = grid
        elif e == 4:
            source = mask_out
        elif dz == 0:
            source = planes.at[e - 2, 1 if dx > 0 else 0]
        else:
            source = tile_out.at[e, 1 if dz > 0 else 0]
        return there, pltpu.make_async_remote_copy(
            src_ref=source,
            dst_ref=landing(e, side),
            send_sem=sem_halo.at[0, e, side],
            recv_sem=sem_halo.at[1, e, side],
            device_id=target,
            device_id_type=MESH,
        )

    for side, (dx, dz) in enumerate(SIDES):
        has_source, _ = near(-dx, -dz)

        @pl.when(jnp.logical_not(has_source))
        def _():
            for e in [e for e in range(5) if side in USED[e]]:
                ref = landing(e, side)
                ref[...] = jnp.zeros(ref.shape, BF16)

    dpad[...] = jnp.zeros(dpad.shape, BF16)
    slots = got.shape[0] * got.shape[1]
    cap = got.shape[1]
    slot = lax.broadcasted_iota(jnp.int32, (1, slots), 1)
    to_slot = lax.broadcasted_iota(jnp.int32, (n_dev, slots), 0) == slot // cap
    counts = jnp.broadcast_to(count[...].astype(F32), (8, n_dev)).astype(BF16)
    counts = dot(counts, jnp.where(to_slot, 1.0, 0.0).astype(BF16))[:1]
    live = lax.rem(slot, cap).astype(F32) < counts
    sent = jnp.concatenate(
        [
            jnp.where(live, feat[0].astype(F32), 0.0),
            jnp.broadcast_to(cell[...].astype(F32), (8, slots)),
            jnp.zeros((LANES - ch - 8, slots), F32),
        ],
        axis=0,
    )
    src[...] = sent.T.astype(BF16).reshape(src.shape)
    for i in range(4):
        wup[i * ch : (i + 1) * ch, :] = jnp.concatenate([w_up[2 * i], w_up[2 * i + 1]], axis=1)
    mask_out[...] = jnp.concatenate([mask_in[0], mask_in[1]], axis=0).astype(F32).astype(BF16)
    stack_forward(w1, a1)
    pl.semaphore_wait(barrier, n_dev - 1)

    def exchange(source, landed, sems):
        def copy(k):
            to = lax.rem(me + k, n_dev)
            return pltpu.make_async_remote_copy(
                src_ref=source(to),
                dst_ref=landed.at[me],
                send_sem=sems.at[0],
                recv_sem=sems.at[1],
                device_id=(to // n_xy, lax.rem(to, n_xy)),
                device_id_type=MESH,
            )

        def finish():
            others = landed.at[pl.ds(0, n_dev - 1)]
            pltpu.make_async_copy(others, others, sems.at[0]).wait()
            pltpu.make_async_copy(others, others, sems.at[1]).wait()

        return copy, finish

    to_copy, to_finish = exchange(lambda to: src.at[to], got, sem_to)
    back_copy, back_finish = exchange(lambda to: slot_grad.at[to], ret, sem_back)
    gather_copy, gather_finish = exchange(lambda to: full_c.at[me], full_c, sem_c)

    def each_device(action):
        def step(k, carry):
            action(k)
            return carry

        lax.fori_loop(1, n_dev, step, 0)

    each_device(lambda k: to_copy(k).start())
    for side in USED[4]:
        there, copy = halo_copy(4, side)
        pl.when(there)(copy.start)
    got[me] = src[me]
    stack_forward(w2, a2)
    to_finish()

    listed = got[...].reshape(slots, LANES)
    half = 4 * LANES
    cells = listed[:, ch : ch + 1].astype(F32)
    owner = lax.broadcasted_iota(jnp.int32, (1, half // 2), 1).astype(F32)
    hot = jnp.where(cells == owner, 1.0, 0.0).astype(BF16)
    grid[...] = dot_tn(listed, hot)[:ch].astype(BF16)
    for side in (0, 1):
        there, copy = halo_copy(0, side)
        pl.when(there)(copy.start)
    column = lax.broadcasted_iota(jnp.int32, (1, half), 1)
    even = lax.rem(column, 2) == 0
    twice = jnp.where(
        lax.broadcasted_iota(jnp.int32, (LANES, 2 * LANES), 0)
        == lax.broadcasted_iota(jnp.int32, (LANES, 2 * LANES), 1) // 2,
        1.0,
        0.0,
    ).astype(BF16)

    def by_parity_of(values):
        wide = jnp.concatenate([dot(values[:, :LANES], twice), dot(values[:, LANES:], twice)], axis=1)
        none = jnp.zeros_like(wide)
        return jnp.concatenate(
            [jnp.where(even, wide, none), jnp.where(even, none, wide)], axis=0
        ).astype(BF16)

    def mask_row(tile, x):
        return jnp.concatenate([tile[x * ny + y : x * ny + y + 1] for y in range(ny)], axis=1)

    def lift(listed_parents, tile):
        up = dot(wup[...], listed_parents)
        result = []
        for a in range(2):
            pieces = []
            for y in range(ny):
                row = (2 * a + y % 2) * ch
                pieces.append(up[row : row + ch, (y // 2) * LANES : (y // 2 + 1) * LANES])
            result.append((jnp.concatenate(pieces, axis=1) * mask_row(tile, a)).astype(BF16))
        return result

    parents = by_parity_of(grid[...])
    own_mask = mask_out[...].astype(F32)

    lane = lax.broadcasted_iota(jnp.int32, (1, LANES), 1)

    def block(value, y):
        return value[:, y * LANES : (y + 1) * LANES]

    def plane_mask(x):
        return mask_row(own_mask, x)

    def cot_plane(x):
        return cot_in[:, x].astype(F32).reshape(ch, width)

    def send_planes(e, fields):
        for x in range(2):
            planes[e - 2, x] = fields[x]
        for side in (0, 1):
            there, copy = halo_copy(e, side)
            pl.when(there)(copy.start)

    def send_edges(e, fields, shift):
        period = len(fields) * ny
        edge = lax.rem(lane, period)
        first = jnp.zeros((ch, LANES), F32)
        last = jnp.zeros((ch, LANES), F32)
        for x, field in enumerate(fields):
            wide = field.astype(F32)
            for y in range(ny):
                here = edge == (shift + x * ny + y) % period
                part = block(wide, y)
                first = jnp.where(here, part[:, :1], first)
                last = jnp.where(here, part[:, LANES - 1 :], last)
        tile_out[e, 0] = first.astype(BF16)
        tile_out[e, 1] = last.astype(BF16)
        for side in (3, 6, 2, 4, 5, 7):
            if side in USED[e]:
                there, copy = halo_copy(e, side)
                pl.when(there)(copy.start)

    def arrive(e, sides):
        for side in sides:
            dx, dz = SIDES[side]
            has_source, _ = near(-dx, -dz)
            _, copy = halo_copy(e, side)
            pl.when(has_source)(copy.wait_recv)

    def tile(e, side):
        return tile_in[e, side - 2].astype(F32)

    def spread(held, xp, field, low, high):
        wide = field.astype(F32)
        held[xp, ch : 2 * ch, :] = field
        for y in range(ny):
            part = block(wide, y)
            at = xp * ny + y
            left = jnp.where(lane == 0, low[:, at : at + 1], pltpu.roll(part, 1, 1))
            right = jnp.where(
                lane == LANES - 1, high[:, at : at + 1], pltpu.roll(part, LANES - 1, 1)
            )
            cols = slice(y * LANES, (y + 1) * LANES)
            held[xp, 0:ch, cols] = left.astype(BF16)
            held[xp, 2 * ch : 3 * ch, cols] = right.astype(BF16)

    def reach(xp, count):
        return [ox for ox in (-1, 0, 1) if 0 <= xp - 1 - ox < count]

    def add(matrix, held, xp, count):
        steps = reach(xp, count)
        low = 3 * ch * (steps[0] + 1)
        product = dot(matrix[low : low + 3 * ch * len(steps), :], held[xp])
        for n, ox in enumerate(steps):
            x = xp - 1 - ox
            for oy in (-1, 0, 1):
                row = (3 * n + oy + 1) * ch
                cols = slice((1 - oy) * LANES, (1 - oy) * LANES + width)
                acc[x, :, cols] += product[row : row + ch]

    def result(count):
        return [acc[x, :, LANES : LANES + width] for x in range(count)]

    def conv(e, fields, held, matrix, meanwhile=()):
        acc[...] = jnp.zeros(acc.shape, F32)
        arrive(e, (3, 6))
        low, high = tile(e, 3), tile(e, 6)
        for xp in (1, 2):
            spread(held, xp, fields[xp - 1], low, high)
            add(matrix, held, xp, 2)
        arrive(e, (0, 1, 2, 4, 5, 7))
        for action in meanwhile:
            action()
        spread(held, 0, plane_in[e - 2, 0], tile(e, 4), tile(e, 7))
        add(matrix, held, 0, 2)
        spread(held, 3, plane_in[e - 2, 1], tile(e, 2), tile(e, 5))
        add(matrix, held, 3, 2)
        return result(2)

    def tap_sums(deltas, held, start):
        for x in range(2):
            dpad[x, :, LANES : LANES + width] = deltas[x]
        total = [jnp.zeros((3 * ch, 3 * ch), F32) for _ in range(3)]
        for xp in range(4):
            steps = reach(xp, 2)
            rows = [
                dpad[xp - 1 - ox, :, (1 - oy) * LANES : (1 - oy) * LANES + width]
                for ox in steps
                for oy in (-1, 0, 1)
            ]
            product = dot_nt(jnp.concatenate(rows, axis=0), held[start + xp])
            for n, ox in enumerate(steps):
                total[ox + 1] = total[ox + 1] + product[3 * ch * n : 3 * ch * (n + 1)]
        return [total[i // 3][(i % 3) * ch : (i % 3 + 1) * ch] for i in range(9)]

    def pack_taps(taps, pack):
        for i in range(9):
            pack[i * ch : (i + 1) * ch, :] = taps[i][:, :LANES]
        for i in range(5):
            second = taps[2 * i + 1][:, LANES:] if i < 4 else jnp.zeros((ch, ch), F32)
            row = (9 + i) * ch
            pack[row : row + ch, :] = jnp.concatenate([taps[2 * i][:, LANES:], second], axis=1)

    class Reduce:
        def __init__(self, pack, wire, in_gz, part, mid, in_xy, full, sems):
            self.pack, self.wire, self.in_gz, self.part = pack, wire, in_gz, part
            self.mid, self.in_xy, self.full, self.sems = mid, in_xy, full, sems
            self.rows = pack.shape[0] // n_gz
            self.sub = self.rows // n_xy

        def copies(self, phase):
            result = []
            for k in range(1, n_gz if phase in (0, 3) else n_xy):
                if phase in (0, 3):
                    to = lax.rem(gz + k, n_gz)
                    target = (to, xy)
                else:
                    to = lax.rem(xy + k, n_xy)
                    target = (gz, to)
                source, landed = [
                    lambda: (self.wire.at[to], self.in_gz.at[k - 1]),
                    lambda: (self.mid.at[to], self.in_xy.at[k - 1]),
                    lambda: (self.full.at[gz, xy], self.full.at[gz, xy]),
                    lambda: (self.full.at[gz], self.full.at[gz]),
                ][phase]()
                result.append(
                    pltpu.make_async_remote_copy(
                        src_ref=source,
                        dst_ref=landed,
                        send_sem=self.sems.at[0, phase, k - 1],
                        recv_sem=self.sems.at[1, phase, k - 1],
                        device_id=target,
                        device_id_type=MESH,
                    )
                )
            return result

        def start(self, phase):
            for copy in self.copies(phase):
                copy.start()

        def finish(self, phase):
            for copy in self.copies(phase):
                copy.wait()

        def begin(self):
            for g in range(n_gz):
                self.wire[g] = self.pack[g * self.rows : (g + 1) * self.rows].astype(BF16)
            self.start(0)

        def second(self):
            self.finish(0)
            total = self.pack[pl.ds(pl.multiple_of(gz * self.rows, 16), self.rows), :]
            for k in range(n_gz - 1):
                total = total + self.in_gz[k].astype(F32)
            for j in range(n_xy):
                piece = total[j * self.sub : (j + 1) * self.sub]
                self.part[j] = piece
                self.mid[j] = piece.astype(BF16)
            self.start(1)

        def third(self):
            self.finish(1)
            total = self.part[xy]
            for k in range(n_xy - 1):
                total = total + self.in_xy[k].astype(F32)
            self.full[gz, xy] = total.astype(BF16)
            self.start(2)

        def fourth(self):
            self.finish(2)
            self.start(3)

        def done(self):
            self.finish(3)
            return self.full[...].reshape(self.rows * n_gz, LANES)

    sum_a = Reduce(pack_a, wire_a, in_a, part_a, mid_a, inx_a, full_a, sem_ra)
    sum_b = Reduce(pack_b, wire_b, in_b, part_b, mid_b, inx_b, full_b, sem_rb)

    lifted = lift(parents, own_mask)
    send_edges(0, lifted, 0)
    stack_backward(w2, b2)
    acc[...] = jnp.zeros(acc.shape, F32)
    arrive(0, (3, 6))
    low, high = tile(0, 3), tile(0, 6)
    for x in range(2):
        spread(s_lift, x + 2, lifted[x], low, high)
        add(a1, s_lift, x + 2, 4)
    arrive(4, (0, 1))
    arrive(0, (0, 1, 2, 4, 5, 7))
    around = []
    for side in (0, 1):
        around.append(mask_halo[side].astype(F32))
        beside = lift(by_parity_of(grid_in[side]), around[side])
        low, high = (tile(0, 4), tile(0, 7)) if side == 0 else (tile(0, 2), tile(0, 5))
        for x in range(2):
            xp = 4 * side + x
            spread(s_lift, xp, beside[x], low, high)
            add(a1, s_lift, xp, 4)
    first = result(4)
    rows = [mask_row(around[0], 1), plane_mask(0), plane_mask(1), mask_row(around[1], 0)]
    acts = [(rows[x] * first[x] * jax.nn.sigmoid(first[x])).astype(BF16) for x in range(4)]
    send_edges(1, acts, 0)
    stack_backward(w1, b1)
    for x in range(2):
        pre1[x] = first[x + 1]
    acc[...] = jnp.zeros(acc.shape, F32)
    arrive(1, (3, 6))
    low, high = tile(1, 3), tile(1, 6)
    for xp in range(4):
        spread(s_act, xp, acts[xp], low, high)
        add(a2, s_act, xp, 2)
    second = result(2)
    deltas = []
    for x in range(2):
        v = second[x]
        sig = jax.nn.sigmoid(v)
        m = plane_mask(x)
        dec[:, x * width : (x + 1) * width] = (m * (v * sig)).astype(BF16)
        slope = sig * (1.0 + v * (1.0 - sig))
        deltas.append((cot_plane(x) * m * slope).astype(BF16))

    used = 14 * ch
    for pack in (pack_a, pack_b):
        if pack.shape[0] > used:
            pack[used:, :] = jnp.zeros((pack.shape[0] - used, LANES), F32)
    send_planes(2, deltas)
    send_edges(2, deltas, 8)
    pack_taps(tap_sums(deltas, s_act, 0), pack_a)
    sum_a.begin()
    back = conv(2, deltas, s_grad, b2)
    deltas = []
    for x in range(2):
        v = pre1[x]
        sig = jax.nn.sigmoid(v)
        slope = sig * (1.0 + v * (1.0 - sig))
        deltas.append((back[x] * plane_mask(x) * slope).astype(BF16))
    send_planes(3, deltas)
    send_edges(3, deltas, 8)
    pack_taps(tap_sums(deltas, s_lift, 1), pack_b)
    sum_b.begin()
    sum_a.second()
    back = conv(3, deltas, s_grad, b1, (sum_b.second, sum_a.third))
    du = [(back[x] * plane_mask(x)).astype(BF16) for x in range(2)]
    stacked = jnp.concatenate(
        [
            jnp.concatenate([block(du[a], 2 * j + b) for j in range(ny // 2)], axis=1)
            for a in range(2)
            for b in range(2)
        ],
        axis=0,
    )
    grad_up = dot_nt(stacked, parents)
    by_parity = dot_tn(wup[...], stacked)
    kept = jnp.where(even, by_parity[:ch], by_parity[ch:])
    paired = kept + pltpu.roll(kept, half - 1, 1)
    parent_grad = jnp.where(even, paired, jnp.zeros_like(paired)).astype(BF16)
    compact = jnp.concatenate(
        [dot_nt(parent_grad[:, h * 2 * LANES : (h + 1) * 2 * LANES], twice) for h in range(2)],
        axis=1,
    )
    compact = jnp.concatenate([compact, jnp.zeros_like(compact)], axis=0).astype(BF16)
    terms = jnp.concatenate([grad_up[:, :ch], grad_up[:, ch:]], axis=0)
    if slots > 8 * ch:
        terms = jnp.concatenate([terms, jnp.zeros((slots - 8 * ch, ch), F32)], axis=0)
    both = jnp.concatenate([dot_nt(hot, compact)[:, :ch], terms], axis=1)
    slot_grad[...] = both.astype(BF16).reshape(slot_grad.shape)
    each_device(lambda k: back_copy(k).start())
    ret[me] = slot_grad[me]
    sum_b.third()
    sum_a.fourth()
    back_finish()
    total = ret[0].astype(F32)
    for d in range(1, n_dev):
        total = total + ret[d].astype(F32)
    full_c[me] = total.astype(BF16)
    each_device(lambda k: gather_copy(k).start())
    sum_b.fourth()
    returned = ret[...].reshape(slots, LANES).astype(F32).T[:ch]
    ret_out[...] = jnp.where(live, returned, 0.0).astype(BF16)
    out_a[...] = sum_a.done()
    gather_finish()
    out_c[...] = full_c[...].reshape(out_c.shape)
    out_b[...] = sum_b.done()
    for e in range(5):
        for side in USED[e]:
            there, copy = halo_copy(e, side)
            pl.when(there)(copy.wait_send)


def finish_kernel(scale, dims, dec, ret, full_a, full_b, full_c, dec_out, ret_out, g1_out, g2_out, gup_out):
    ch, ny = dims
    width = ny * LANES
    for x in range(2):
        plane = dec[:, x * width : (x + 1) * width].astype(F32)
        dec_out[:, x] = plane.reshape(ch, ny, LANES).astype(BF16)
    ret_out[0] = ret[...]
    for full, out in ((full_b, g1_out), (full_a, g2_out)):
        for i in range(9):
            tile = full[i * ch : (i + 1) * ch].astype(F32) * scale
            out[3 * i] = tile[:, :ch]
            out[3 * i + 1] = tile[:, ch:]
            pair = full[(9 + i // 2) * ch : (10 + i // 2) * ch].astype(F32) * scale
            out[3 * i + 2] = pair[:, :ch] if i % 2 == 0 else pair[:, ch:]
    for p in range(4):
        for e in range(2):
            row = (4 * e + p) * ch
            gup_out[2 * p + e] = full_c[row : row + ch].astype(F32)[:, ch:] * scale


def local(
    parent_feat, parent_cell, send_count, up_weight, conv_one, conv_two, child_mask, cotangent
):
    ch, size_x, ny, size_z = cotangent.shape
    n_gz, n_xy = lax.axis_size("gz"), lax.axis_size("xy")
    n_dev = n_gz * n_xy
    slot_total = parent_feat.shape[2]
    cap = slot_total // n_dev
    voxels = size_x * ny * size_z
    width = ny * size_z
    unit = n_dev * 16
    rows_a = -(-14 * ch // unit) * unit
    assert 8 * ch <= slot_total

    def reduce_scratch(rows):
        per = rows // n_gz
        sub = per // n_xy
        return [
            pltpu.VMEM((rows, LANES), F32),
            pltpu.VMEM((n_gz, per, LANES), BF16),
            pltpu.VMEM((n_gz - 1, per, LANES), BF16),
            pltpu.VMEM((n_xy, sub, LANES), F32),
            pltpu.VMEM((n_xy, sub, LANES), BF16),
            pltpu.VMEM((n_xy - 1, sub, LANES), BF16),
            pltpu.VMEM((n_gz, n_xy, sub, LANES), BF16),
        ]

    vmem = pl.BlockSpec(memory_space=pltpu.VMEM)
    most = max(n_gz, n_xy) - 1
    dma = pltpu.SemaphoreType.DMA
    dec, ret, full_a, full_b, full_c = pl.pallas_call(
        functools.partial(all_kernel, (n_gz, n_xy, ch, ny)),
        out_shape=(
            jax.ShapeDtypeStruct((ch, voxels), BF16),
            jax.ShapeDtypeStruct((ch, slot_total), BF16),
            jax.ShapeDtypeStruct((rows_a, LANES), BF16),
            jax.ShapeDtypeStruct((rows_a, LANES), BF16),
            jax.ShapeDtypeStruct((slot_total, LANES), BF16),
        ),
        in_specs=[vmem] * 8,
        out_specs=(vmem,) * 5,
        scratch_shapes=[
            pltpu.VMEM((n_dev, cap, LANES), BF16),
            pltpu.VMEM((4 * ch, 2 * ch), BF16),
            pltpu.VMEM((n_dev, cap, LANES), BF16),
            pltpu.VMEM((n_dev, cap, LANES), BF16),
            pltpu.VMEM((n_dev, cap, LANES), BF16),
            pltpu.VMEM((9 * ch, 3 * ch), BF16),
            pltpu.VMEM((9 * ch, 3 * ch), BF16),
            pltpu.VMEM((9 * ch, 3 * ch), BF16),
            pltpu.VMEM((9 * ch, 3 * ch), BF16),
            pltpu.VMEM((ch, 2 * LANES), BF16),
            pltpu.VMEM((2, ch, 2 * LANES), BF16),
            pltpu.VMEM((2 * ny, LANES), BF16),
            pltpu.VMEM((2, 2 * ny, LANES), BF16),
            pltpu.VMEM((2, 2, ch, width), BF16),
            pltpu.VMEM((2, 2, ch, width), BF16),
            pltpu.VMEM((4, 2, ch, LANES), BF16),
            pltpu.VMEM((4, 6, ch, LANES), BF16),
            pltpu.VMEM((6, 3 * ch, width), BF16),
            pltpu.VMEM((4, 3 * ch, width), BF16),
            pltpu.VMEM((4, 3 * ch, width), BF16),
            pltpu.VMEM((4, ch, width + 2 * LANES), F32),
            pltpu.VMEM((2, ch, width + 2 * LANES), BF16),
            pltpu.VMEM((2, ch, width), F32),
            *reduce_scratch(rows_a),
            *reduce_scratch(rows_a),
            pltpu.VMEM((n_dev, cap, LANES), BF16),
            dma((2,)),
            dma((2,)),
            dma((2, 5, 8)),
            dma((2, 4, most)),
            dma((2, 4, most)),
            dma((2,)),
        ],
        compiler_params=pltpu.CompilerParams(
            collective_id=0, has_side_effects=True, vmem_limit_bytes=56 * 1024 * 1024
        ),
    )(parent_feat, parent_cell, send_count, up_weight, conv_one, conv_two, child_mask, cotangent)
    scale = 1.0 / math.sqrt(size_x * n_xy * ny * size_z * n_gz)
    return pl.pallas_call(
        functools.partial(finish_kernel, scale, (ch, ny)),
        out_shape=(
            jax.ShapeDtypeStruct(cotangent.shape, BF16),
            jax.ShapeDtypeStruct((1, ch, slot_total), BF16),
            jax.ShapeDtypeStruct((27, ch, ch), F32),
            jax.ShapeDtypeStruct((27, ch, ch), F32),
            jax.ShapeDtypeStruct((8, ch, ch), F32),
        ),
        in_specs=[vmem] * 5,
        out_specs=(vmem,) * 5,
    )(dec, ret, full_a, full_b, full_c)


def solution(mesh):
    placed = (
        P(("gz", "xy"), None, None),
        P(("gz", "xy"), None),
        P(("gz", "xy"), None),
        P(),
        P(),
        P(),
        P("xy", None, "gz"),
        P(None, "xy", None, "gz"),
    )
    return jax.shard_map(
        local,
        mesh=mesh,
        in_specs=placed,
        out_specs=(P(None, "xy", None, "gz"), P(("gz", "xy"), None, None), P(), P(), P()),
        check_vma=False,
    )
```

```python
import functools
import math

import jax
import jax.numpy as jnp
from jax import lax
from jax.experimental import pallas as pl
from jax.experimental.pallas import tpu as pltpu
from jax.sharding import PartitionSpec as P

MESH = pl.DeviceIdType.MESH
F32 = jnp.float32
BF16 = jnp.bfloat16
LANES = 128
USED = [range(8), (3, 6), range(8), range(8), (0, 1)]
SIDES = [(1, 0), (-1, 0), (-1, 1), (0, 1), (1, 1), (-1, -1), (0, -1), (1, -1)]


def dot(a, b):
    return jnp.dot(a, b, preferred_element_type=F32)


def dot_nt(a, b):
    return lax.dot_general(a, b, (((1,), (1,)), ((), ())), preferred_element_type=F32)


def dot_tn(a, b):
    return lax.dot_general(a, b, (((0,), (0,)), ((), ())), preferred_element_type=F32)


def all_kernel(
    dims,
    feat, cell, count, w_up, w1_in, w2_in, mask_in, cot_hbm,
    dec, ret_out, out_a, out_b, out_c,
    w1, w2, cot_in, sem_in,
    src, wup, got, slot_grad, ret,
    a1, b1, a2, b2,
    grid, grid_in, mask_out, mask_halo,
    planes, plane_in, tile_out, tile_in,
    s_lift, s_act, s_grad, acc, dpad, pre1,
    pack_a, wire_a, in_a, part_a, mid_a, inx_a, full_a,
    pack_b, wire_b, in_b, part_b, mid_b, inx_b, full_b,
    full_c,
    sem_to, sem_back, sem_halo, sem_ra, sem_rb, sem_c,
):
    n_gz, n_xy, ch, ny = dims
    n_dev = n_gz * n_xy
    width = ny * LANES
    gz = lax.axis_index("gz")
    xy = lax.axis_index("xy")
    me = gz * n_xy + xy

    barrier = pltpu.get_barrier_semaphore()

    def greet(k, carry):
        to = lax.rem(me + k, n_dev)
        pl.semaphore_signal(
            barrier, inc=1, device_id=(lax.div(to, n_xy), lax.rem(to, n_xy)), device_id_type=MESH
        )
        return carry

    loads = [
        pltpu.make_async_copy(source, into, sem_in.at[n])
        for n, (source, into) in enumerate(((w1_in, w1), (w2_in, w2), (cot_hbm, cot_in)))
    ]
    for load in loads:
        load.start()
    lax.fori_loop(1, n_dev, greet, 0)

    def stack_forward(w, into):
        def step(i, carry):
            rows = pl.ds(pl.multiple_of(i * ch, ch), ch)
            into[rows, :] = jnp.concatenate([w[3 * i + t] for t in range(3)], axis=1)
            return carry

        lax.fori_loop(0, 9, step, 0)

    def stack_backward(w, into):
        def step(i, carry):
            rows = pl.ds(pl.multiple_of(i * ch, ch), ch)
            into[rows, :] = jnp.concatenate(
                [w[26 - 3 * i - t].astype(F32).T.astype(BF16) for t in range(3)], axis=1
            )
            return carry

        lax.fori_loop(0, 9, step, 0)

    def near(dx, dz):
        x, z = xy + dx, gz + dz
        there = (x >= 0) & (x < n_xy) & (z >= 0) & (z < n_gz)
        return there, (z, x)

    def landing(e, side):
        dx, dz = SIDES[side]
        if dz != 0:
            return tile_in.at[e, side - 2]
        return {0: grid_in, 4: mask_halo}[e].at[side] if e in (0, 4) else plane_in.at[e - 2, side]

    def halo_copy(e, side):
        dx, dz = SIDES[side]
        there, target = near(dx, dz)
        if e == 0 and dz == 0:
            source = grid
        elif e == 4:
            source = mask_out
        elif dz == 0:
            source = planes.at[e - 2, 1 if dx > 0 else 0]
        else:
            source = tile_out.at[e, 1 if dz > 0 else 0]
        return there, pltpu.make_async_remote_copy(
            src_ref=source,
            dst_ref=landing(e, side),
            send_sem=sem_halo.at[0, e, side],
            recv_sem=sem_halo.at[1, e, side],
            device_id=target,
            device_id_type=MESH,
        )

    for side, (dx, dz) in enumerate(SIDES):
        has_source, _ = near(-dx, -dz)

        @pl.when(jnp.logical_not(has_source))
        def _():
            for e in [e for e in range(5) if side in USED[e]]:
                ref = landing(e, side)
                ref[...] = jnp.zeros(ref.shape, BF16)

    dpad[...] = jnp.zeros(dpad.shape, BF16)
    slots = got.shape[0] * got.shape[1]
    cap = got.shape[1]
    slot = lax.broadcasted_iota(jnp.int32, (1, slots), 1)
    to_slot = lax.broadcasted_iota(jnp.int32, (n_dev, slots), 0) == slot // cap
    counts = jnp.broadcast_to(count[...].astype(F32), (8, n_dev)).astype(BF16)
    counts = dot(counts, jnp.where(to_slot, 1.0, 0.0).astype(BF16))[:1]
    live = lax.rem(slot, cap).astype(F32) < counts
    sent = jnp.concatenate(
        [
            jnp.where(live, feat[0].astype(F32), 0.0),
            jnp.broadcast_to(cell[...].astype(F32), (8, slots)),
            jnp.zeros((LANES - ch - 8, slots), F32),
        ],
        axis=0,
    )
    src[...] = sent.T.astype(BF16).reshape(src.shape)
    for i in range(4):
        wup[i * ch : (i + 1) * ch, :] = jnp.concatenate([w_up[2 * i], w_up[2 * i + 1]], axis=1)
    mask_out[...] = jnp.concatenate([mask_in[0], mask_in[1]], axis=0).astype(F32).astype(BF16)
    loads[0].wait()
    stack_forward(w1, a1)
    pl.semaphore_wait(barrier, n_dev - 1)

    def exchange(source, landed, sems):
        def copy(k):
            to = lax.rem(me + k, n_dev)
            return pltpu.make_async_remote_copy(
                src_ref=source(to),
                dst_ref=landed.at[me],
                send_sem=sems.at[0],
                recv_sem=sems.at[1],
                device_id=(lax.div(to, n_xy), lax.rem(to, n_xy)),
                device_id_type=MESH,
            )

        def finish():
            others = landed.at[pl.ds(0, n_dev - 1)]
            pltpu.make_async_copy(others, others, sems.at[0]).wait()
            pltpu.make_async_copy(others, others, sems.at[1]).wait()

        return copy, finish

    to_copy, to_finish = exchange(lambda to: src.at[to], got, sem_to)
    back_copy, back_finish = exchange(lambda to: slot_grad.at[to], ret, sem_back)
    gather_copy, gather_finish = exchange(lambda to: full_c.at[me], full_c, sem_c)

    def each_device(action):
        def step(k, carry):
            action(k)
            return carry

        lax.fori_loop(1, n_dev, step, 0)

    each_device(lambda k: to_copy(k).start())
    for side in USED[4]:
        there, copy = halo_copy(4, side)
        pl.when(there)(copy.start)
    got[me] = src[me]
    loads[1].wait()
    stack_forward(w2, a2)
    loads[2].wait()
    to_finish()

    listed = got[...].reshape(slots, LANES)
    half = 4 * LANES
    cells = listed[:, ch : ch + 1].astype(F32)
    owner = lax.broadcasted_iota(jnp.int32, (1, half // 2), 1).astype(F32)
    hot = jnp.where(cells == owner, 1.0, 0.0).astype(BF16)
    grid[...] = dot_tn(listed, hot)[:ch].astype(BF16)
    for side in (0, 1):
        there, copy = halo_copy(0, side)
        pl.when(there)(copy.start)
    column = lax.broadcasted_iota(jnp.int32, (1, half), 1)
    even = lax.rem(column, 2) == 0
    twice = jnp.where(
        lax.broadcasted_iota(jnp.int32, (LANES, 2 * LANES), 0)
        == lax.broadcasted_iota(jnp.int32, (LANES, 2 * LANES), 1) // 2,
        1.0,
        0.0,
    ).astype(BF16)

    def by_parity_of(values):
        wide = jnp.concatenate([dot(values[:, :LANES], twice), dot(values[:, LANES:], twice)], axis=1)
        none = jnp.zeros_like(wide)
        return jnp.concatenate(
            [jnp.where(even, wide, none), jnp.where(even, none, wide)], axis=0
        ).astype(BF16)

    def mask_row(tile, x):
        return jnp.concatenate([tile[x * ny + y : x * ny + y + 1] for y in range(ny)], axis=1)

    def lift(listed_parents, tile):
        up = dot(wup[...], listed_parents)
        result = []
        for a in range(2):
            pieces = []
            for y in range(ny):
                row = (2 * a + y % 2) * ch
                pieces.append(up[row : row + ch, (y // 2) * LANES : (y // 2 + 1) * LANES])
            result.append((jnp.concatenate(pieces, axis=1) * mask_row(tile, a)).astype(BF16))
        return result

    parents = by_parity_of(grid[...])
    own_mask = mask_out[...].astype(F32)

    lane = lax.broadcasted_iota(jnp.int32, (1, LANES), 1)

    def block(value, y):
        return value[:, y * LANES : (y + 1) * LANES]

    def plane_mask(x):
        return mask_row(own_mask, x)

    def cot_plane(x):
        return cot_in[:, x].astype(F32).reshape(ch, width)

    def send_planes(e, fields):
        for x in range(2):
            planes[e - 2, x] = fields[x]
        for side in (0, 1):
            there, copy = halo_copy(e, side)
            pl.when(there)(copy.start)

    def send_edges(e, fields, shift):
        period = len(fields) * ny
        edge = lax.rem(lane, period)
        first = jnp.zeros((ch, LANES), F32)
        last = jnp.zeros((ch, LANES), F32)
        for x, field in enumerate(fields):
            wide = field.astype(F32)
            for y in range(ny):
                here = edge == (shift + x * ny + y) % period
                part = block(wide, y)
                first = jnp.where(here, part[:, :1], first)
                last = jnp.where(here, part[:, LANES - 1 :], last)
        tile_out[e, 0] = first.astype(BF16)
        tile_out[e, 1] = last.astype(BF16)
        for side in (3, 6, 2, 4, 5, 7):
            if side in USED[e]:
                there, copy = halo_copy(e, side)
                pl.when(there)(copy.start)

    def arrive(e, sides):
        for side in sides:
            dx, dz = SIDES[side]
            has_source, _ = near(-dx, -dz)
            _, copy = halo_copy(e, side)
            pl.when(has_source)(copy.wait_recv)

    def tile(e, side):
        return tile_in[e, side - 2].astype(F32)

    def spread(held, xp, field, low, high):
        wide = field.astype(F32)
        held[xp, ch : 2 * ch, :] = field
        for y in range(ny):
            part = block(wide, y)
            at = xp * ny + y
            left = jnp.where(lane == 0, low[:, at : at + 1], pltpu.roll(part, 1, 1))
            right = jnp.where(
                lane == LANES - 1, high[:, at : at + 1], pltpu.roll(part, LANES - 1, 1)
            )
            cols = slice(y * LANES, (y + 1) * LANES)
            held[xp, 0:ch, cols] = left.astype(BF16)
            held[xp, 2 * ch : 3 * ch, cols] = right.astype(BF16)

    def reach(xp, count):
        return [ox for ox in (-1, 0, 1) if 0 <= xp - 1 - ox < count]

    def add(matrix, held, xp, count):
        steps = reach(xp, count)
        low = 3 * ch * (steps[0] + 1)
        product = dot(matrix[low : low + 3 * ch * len(steps), :], held[xp])
        for n, ox in enumerate(steps):
            x = xp - 1 - ox
            for oy in (-1, 0, 1):
                row = (3 * n + oy + 1) * ch
                cols = slice((1 - oy) * LANES, (1 - oy) * LANES + width)
                acc[x, :, cols] += product[row : row + ch]

    def result(count):
        return [acc[x, :, LANES : LANES + width] for x in range(count)]

    def conv(e, fields, held, matrix, meanwhile=()):
        acc[...] = jnp.zeros(acc.shape, F32)
        arrive(e, (3, 6))
        low, high = tile(e, 3), tile(e, 6)
        for xp in (1, 2):
            spread(held, xp, fields[xp - 1], low, high)
            add(matrix, held, xp, 2)
        arrive(e, (0, 1, 2, 4, 5, 7))
        for action in meanwhile:
            action()
        spread(held, 0, plane_in[e - 2, 0], tile(e, 4), tile(e, 7))
        add(matrix, held, 0, 2)
        spread(held, 3, plane_in[e - 2, 1], tile(e, 2), tile(e, 5))
        add(matrix, held, 3, 2)
        return result(2)

    def tap_sums(deltas, held, start):
        for x in range(2):
            dpad[x, :, LANES : LANES + width] = deltas[x]
        total = [jnp.zeros((3 * ch, 3 * ch), F32) for _ in range(3)]
        for xp in range(4):
            steps = reach(xp, 2)
            rows = [
                dpad[xp - 1 - ox, :, (1 - oy) * LANES : (1 - oy) * LANES + width]
                for ox in steps
                for oy in (-1, 0, 1)
            ]
            product = dot_nt(jnp.concatenate(rows, axis=0), held[start + xp])
            for n, ox in enumerate(steps):
                total[ox + 1] = total[ox + 1] + product[3 * ch * n : 3 * ch * (n + 1)]
        return [total[i // 3][(i % 3) * ch : (i % 3 + 1) * ch] for i in range(9)]

    def pack_taps(taps, pack):
        for i in range(9):
            pack[i * ch : (i + 1) * ch, :] = taps[i][:, :LANES]
        for i in range(5):
            second = taps[2 * i + 1][:, LANES:] if i < 4 else jnp.zeros((ch, ch), F32)
            row = (9 + i) * ch
            pack[row : row + ch, :] = jnp.concatenate([taps[2 * i][:, LANES:], second], axis=1)

    class Reduce:
        def __init__(self, pack, wire, in_gz, part, mid, in_xy, full, sems):
            self.pack, self.wire, self.in_gz, self.part = pack, wire, in_gz, part
            self.mid, self.in_xy, self.full, self.sems = mid, in_xy, full, sems
            self.rows = pack.shape[0] // n_gz
            self.sub = self.rows // n_xy

        def copies(self, phase):
            result = []
            for k in range(1, n_gz if phase in (0, 3) else n_xy):
                if phase in (0, 3):
                    to = lax.rem(gz + k, n_gz)
                    target = (to, xy)
                else:
                    to = lax.rem(xy + k, n_xy)
                    target = (gz, to)
                source, landed = [
                    lambda: (self.wire.at[to], self.in_gz.at[k - 1]),
                    lambda: (self.mid.at[to], self.in_xy.at[k - 1]),
                    lambda: (self.full.at[gz, xy], self.full.at[gz, xy]),
                    lambda: (self.full.at[gz], self.full.at[gz]),
                ][phase]()
                result.append(
                    pltpu.make_async_remote_copy(
                        src_ref=source,
                        dst_ref=landed,
                        send_sem=self.sems.at[0, phase, k - 1],
                        recv_sem=self.sems.at[1, phase, k - 1],
                        device_id=target,
                        device_id_type=MESH,
                    )
                )
            return result

        def start(self, phase):
            for copy in self.copies(phase):
                copy.start()

        def finish(self, phase):
            for copy in self.copies(phase):
                copy.wait()

        def begin(self):
            for g in range(n_gz):
                self.wire[g] = self.pack[g * self.rows : (g + 1) * self.rows].astype(BF16)
            self.start(0)

        def second(self):
            self.finish(0)
            total = self.pack[pl.ds(pl.multiple_of(gz * self.rows, 16), self.rows), :]
            for k in range(n_gz - 1):
                total = total + self.in_gz[k].astype(F32)
            for j in range(n_xy):
                piece = total[j * self.sub : (j + 1) * self.sub]
                self.part[j] = piece
                self.mid[j] = piece.astype(BF16)
            self.start(1)

        def third(self):
            self.finish(1)
            total = self.part[xy]
            for k in range(n_xy - 1):
                total = total + self.in_xy[k].astype(F32)
            self.full[gz, xy] = total.astype(BF16)
            self.start(2)

        def fourth(self):
            self.finish(2)
            self.start(3)

        def done(self):
            self.finish(3)
            return self.full[...].reshape(self.rows * n_gz, LANES)

    sum_a = Reduce(pack_a, wire_a, in_a, part_a, mid_a, inx_a, full_a, sem_ra)
    sum_b = Reduce(pack_b, wire_b, in_b, part_b, mid_b, inx_b, full_b, sem_rb)

    lifted = lift(parents, own_mask)
    send_edges(0, lifted, 0)
    stack_backward(w2, b2)
    acc[...] = jnp.zeros(acc.shape, F32)
    arrive(0, (3, 6))
    low, high = tile(0, 3), tile(0, 6)
    for x in range(2):
        spread(s_lift, x + 2, lifted[x], low, high)
        add(a1, s_lift, x + 2, 4)
    arrive(4, (0, 1))
    arrive(0, (0, 1, 2, 4, 5, 7))
    around = []
    for side in (0, 1):
        around.append(mask_halo[side].astype(F32))
        beside = lift(by_parity_of(grid_in[side]), around[side])
        low, high = (tile(0, 4), tile(0, 7)) if side == 0 else (tile(0, 2), tile(0, 5))
        for x in range(2):
            xp = 4 * side + x
            spread(s_lift, xp, beside[x], low, high)
            add(a1, s_lift, xp, 4)
    first = result(4)
    rows = [mask_row(around[0], 1), plane_mask(0), plane_mask(1), mask_row(around[1], 0)]
    acts = [(rows[x] * first[x] * jax.nn.sigmoid(first[x])).astype(BF16) for x in range(4)]
    send_edges(1, acts, 0)
    stack_backward(w1, b1)
    for x in range(2):
        pre1[x] = first[x + 1]
    acc[...] = jnp.zeros(acc.shape, F32)
    arrive(1, (3, 6))
    low, high = tile(1, 3), tile(1, 6)
    for xp in range(4):
        spread(s_act, xp, acts[xp], low, high)
        add(a2, s_act, xp, 2)
    second = result(2)
    deltas = []
    for x in range(2):
        v = second[x]
        sig = jax.nn.sigmoid(v)
        m = plane_mask(x)
        dec[:, x * width : (x + 1) * width] = (m * (v * sig)).astype(BF16)
        slope = sig * (1.0 + v * (1.0 - sig))
        deltas.append((cot_plane(x) * m * slope).astype(BF16))

    used = 14 * ch
    for pack in (pack_a, pack_b):
        if pack.shape[0] > used:
            pack[used:, :] = jnp.zeros((pack.shape[0] - used, LANES), F32)
    send_planes(2, deltas)
    send_edges(2, deltas, 8)
    pack_taps(tap_sums(deltas, s_act, 0), pack_a)
    sum_a.begin()
    back = conv(2, deltas, s_grad, b2, (sum_a.second,))
    deltas = []
    for x in range(2):
        v = pre1[x]
        sig = jax.nn.sigmoid(v)
        slope = sig * (1.0 + v * (1.0 - sig))
        deltas.append((back[x] * plane_mask(x) * slope).astype(BF16))
    send_planes(3, deltas)
    send_edges(3, deltas, 8)
    pack_taps(tap_sums(deltas, s_lift, 1), pack_b)
    sum_b.begin()
    sum_a.third()
    back = conv(3, deltas, s_grad, b1, (sum_b.second, sum_a.fourth))
    du = [(back[x] * plane_mask(x)).astype(BF16) for x in range(2)]
    stacked = jnp.concatenate(
        [
            jnp.concatenate([block(du[a], 2 * j + b) for j in range(ny // 2)], axis=1)
            for a in range(2)
            for b in range(2)
        ],
        axis=0,
    )
    grad_up = dot_nt(stacked, parents)
    by_parity = dot_tn(wup[...], stacked)
    kept = jnp.where(even, by_parity[:ch], by_parity[ch:])
    paired = kept + pltpu.roll(kept, half - 1, 1)
    parent_grad = jnp.where(even, paired, jnp.zeros_like(paired)).astype(BF16)
    compact = jnp.concatenate(
        [dot_nt(parent_grad[:, h * 2 * LANES : (h + 1) * 2 * LANES], twice) for h in range(2)],
        axis=1,
    )
    compact = jnp.concatenate([compact, jnp.zeros_like(compact)], axis=0).astype(BF16)
    terms = jnp.concatenate([grad_up[:, :ch], grad_up[:, ch:]], axis=0)
    if slots > 8 * ch:
        terms = jnp.concatenate([terms, jnp.zeros((slots - 8 * ch, ch), F32)], axis=0)
    both = jnp.concatenate([dot_nt(hot, compact)[:, :ch], terms], axis=1)
    slot_grad[...] = both.astype(BF16).reshape(slot_grad.shape)
    each_device(lambda k: back_copy(k).start())
    ret[me] = slot_grad[me]
    sum_b.third()
    back_finish()
    sum_b.fourth()
    total = ret[0].astype(F32)
    for d in range(1, n_dev):
        total = total + ret[d].astype(F32)
    full_c[me] = total.astype(BF16)
    each_device(lambda k: gather_copy(k).start())
    returned = ret[...].reshape(slots, LANES).astype(F32).T[:ch]
    ret_out[...] = jnp.where(live, returned, 0.0).astype(BF16)
    out_a[...] = sum_a.done()
    gather_finish()
    out_c[...] = full_c[...].reshape(out_c.shape)
    out_b[...] = sum_b.done()
    for e in range(5):
        for side in USED[e]:
            there, copy = halo_copy(e, side)
            pl.when(there)(copy.wait_send)


def finish_kernel(scale, dims, dec, ret, full_a, full_b, full_c, dec_out, ret_out, g1_out, g2_out, gup_out):
    ch, ny = dims
    width = ny * LANES
    for x in range(2):
        plane = dec[:, x * width : (x + 1) * width].astype(F32)
        dec_out[:, x] = plane.reshape(ch, ny, LANES).astype(BF16)
    ret_out[0] = ret[...]
    for full, out in ((full_b, g1_out), (full_a, g2_out)):
        for i in range(9):
            tile = full[i * ch : (i + 1) * ch].astype(F32) * scale
            out[3 * i] = tile[:, :ch]
            out[3 * i + 1] = tile[:, ch:]
            pair = full[(9 + i // 2) * ch : (10 + i // 2) * ch].astype(F32) * scale
            out[3 * i + 2] = pair[:, :ch] if i % 2 == 0 else pair[:, ch:]
    for p in range(4):
        for e in range(2):
            row = (4 * e + p) * ch
            gup_out[2 * p + e] = full_c[row : row + ch].astype(F32)[:, ch:] * scale


def local(
    parent_feat, parent_cell, send_count, up_weight, conv_one, conv_two, child_mask, cotangent
):
    ch, size_x, ny, size_z = cotangent.shape
    n_gz, n_xy = lax.axis_size("gz"), lax.axis_size("xy")
    n_dev = n_gz * n_xy
    slot_total = parent_feat.shape[2]
    cap = slot_total // n_dev
    voxels = size_x * ny * size_z
    width = ny * size_z
    unit = n_dev * 16
    rows_a = -(-14 * ch // unit) * unit
    assert 8 * ch <= slot_total

    def reduce_scratch(rows):
        per = rows // n_gz
        sub = per // n_xy
        return [
            pltpu.VMEM((rows, LANES), F32),
            pltpu.VMEM((n_gz, per, LANES), BF16),
            pltpu.VMEM((n_gz - 1, per, LANES), BF16),
            pltpu.VMEM((n_xy, sub, LANES), F32),
            pltpu.VMEM((n_xy, sub, LANES), BF16),
            pltpu.VMEM((n_xy - 1, sub, LANES), BF16),
            pltpu.VMEM((n_gz, n_xy, sub, LANES), BF16),
        ]

    vmem = pl.BlockSpec(memory_space=pltpu.VMEM)
    most = max(n_gz, n_xy) - 1
    dma = pltpu.SemaphoreType.DMA
    dec, ret, full_a, full_b, full_c = pl.pallas_call(
        functools.partial(all_kernel, (n_gz, n_xy, ch, ny)),
        out_shape=(
            jax.ShapeDtypeStruct((ch, voxels), BF16),
            jax.ShapeDtypeStruct((ch, slot_total), BF16),
            jax.ShapeDtypeStruct((rows_a, LANES), BF16),
            jax.ShapeDtypeStruct((rows_a, LANES), BF16),
            jax.ShapeDtypeStruct((slot_total, LANES), BF16),
        ),
        in_specs=[vmem] * 4 + [pl.BlockSpec(memory_space=pl.ANY)] * 2 + [vmem, pl.BlockSpec(memory_space=pl.ANY)],
        out_specs=(vmem,) * 5,
        scratch_shapes=[
            pltpu.VMEM(conv_one.shape, BF16),
            pltpu.VMEM(conv_two.shape, BF16),
            pltpu.VMEM(cotangent.shape, BF16),
            dma((3,)),
            pltpu.VMEM((n_dev, cap, LANES), BF16),
            pltpu.VMEM((4 * ch, 2 * ch), BF16),
            pltpu.VMEM((n_dev, cap, LANES), BF16),
            pltpu.VMEM((n_dev, cap, LANES), BF16),
            pltpu.VMEM((n_dev, cap, LANES), BF16),
            pltpu.VMEM((9 * ch, 3 * ch), BF16),
            pltpu.VMEM((9 * ch, 3 * ch), BF16),
            pltpu.VMEM((9 * ch, 3 * ch), BF16),
            pltpu.VMEM((9 * ch, 3 * ch), BF16),
            pltpu.VMEM((ch, 2 * LANES), BF16),
            pltpu.VMEM((2, ch, 2 * LANES), BF16),
            pltpu.VMEM((2 * ny, LANES), BF16),
            pltpu.VMEM((2, 2 * ny, LANES), BF16),
            pltpu.VMEM((2, 2, ch, width), BF16),
            pltpu.VMEM((2, 2, ch, width), BF16),
            pltpu.VMEM((4, 2, ch, LANES), BF16),
            pltpu.VMEM((4, 6, ch, LANES), BF16),
            pltpu.VMEM((6, 3 * ch, width), BF16),
            pltpu.VMEM((4, 3 * ch, width), BF16),
            pltpu.VMEM((4, 3 * ch, width), BF16),
            pltpu.VMEM((4, ch, width + 2 * LANES), F32),
            pltpu.VMEM((2, ch, width + 2 * LANES), BF16),
            pltpu.VMEM((2, ch, width), F32),
            *reduce_scratch(rows_a),
            *reduce_scratch(rows_a),
            pltpu.VMEM((n_dev, cap, LANES), BF16),
            dma((2,)),
            dma((2,)),
            dma((2, 5, 8)),
            dma((2, 4, most)),
            dma((2, 4, most)),
            dma((2,)),
        ],
        compiler_params=pltpu.CompilerParams(
            collective_id=0, has_side_effects=True, vmem_limit_bytes=56 * 1024 * 1024
        ),
    )(parent_feat, parent_cell, send_count, up_weight, conv_one, conv_two, child_mask, cotangent)
    scale = 1.0 / math.sqrt(size_x * n_xy * ny * size_z * n_gz)
    return pl.pallas_call(
        functools.partial(finish_kernel, scale, (ch, ny)),
        out_shape=(
            jax.ShapeDtypeStruct(cotangent.shape, BF16),
            jax.ShapeDtypeStruct((1, ch, slot_total), BF16),
            jax.ShapeDtypeStruct((27, ch, ch), F32),
            jax.ShapeDtypeStruct((27, ch, ch), F32),
            jax.ShapeDtypeStruct((8, ch, ch), F32),
        ),
        in_specs=[vmem] * 5,
        out_specs=(vmem,) * 5,
    )(dec, ret, full_a, full_b, full_c)


def solution(mesh):
    placed = (
        P(("gz", "xy"), None, None),
        P(("gz", "xy"), None),
        P(("gz", "xy"), None),
        P(),
        P(),
        P(),
        P("xy", None, "gz"),
        P(None, "xy", None, "gz"),
    )
    return jax.shard_map(
        local,
        mesh=mesh,
        in_specs=placed,
        out_specs=(P(None, "xy", None, "gz"), P(("gz", "xy"), None, None), P(), P(), P()),
        check_vma=False,
    )
```

```python
import functools
import math

import jax
import jax.numpy as jnp
from jax import lax
from jax.experimental import pallas as pl
from jax.experimental.pallas import tpu as pltpu
from jax.sharding import PartitionSpec as P

MESH = pl.DeviceIdType.MESH
F32 = jnp.float32
BF16 = jnp.bfloat16
LANES = 128
USED = [range(8), (3, 6), range(8), range(8), (0, 1)]
SIDES = [(1, 0), (-1, 0), (-1, 1), (0, 1), (1, 1), (-1, -1), (0, -1), (1, -1)]


def dot(a, b):
    return jnp.dot(a, b, preferred_element_type=F32)


def dot_nt(a, b):
    return lax.dot_general(a, b, (((1,), (1,)), ((), ())), preferred_element_type=F32)


def dot_tn(a, b):
    return lax.dot_general(a, b, (((0,), (0,)), ((), ())), preferred_element_type=F32)


def all_kernel(
    dims,
    feat, cell, count, w_up, w1_in, w2_in, mask_in, cot_hbm,
    dec, ret_out, out_a, out_b, out_c,
    w1, w2, cot_in, sem_in,
    src, wup, got, slot_grad, ret,
    a1, b1, a2, b2,
    grid, grid_in, mask_out, mask_halo,
    planes, plane_in, tile_out, tile_in,
    s_lift, s_act, s_grad, acc, dpad, pre1,
    pack_a, wire_a, in_a, part_a, mid_a, inx_a, full_a,
    pack_b, wire_b, in_b, part_b, mid_b, inx_b, full_b,
    full_c,
    sem_to, sem_back, sem_halo, sem_ra, sem_rb, sem_c,
):
    n_gz, n_xy, ch, ny = dims
    n_dev = n_gz * n_xy
    width = ny * LANES
    gz = lax.axis_index("gz")
    xy = lax.axis_index("xy")
    me = gz * n_xy + xy

    barrier = pltpu.get_barrier_semaphore()

    def greet(k, carry):
        to = lax.rem(me + k, n_dev)
        pl.semaphore_signal(
            barrier, inc=1, device_id=(lax.div(to, n_xy), lax.rem(to, n_xy)), device_id_type=MESH
        )
        return carry

    loads = [
        pltpu.make_async_copy(source, into, sem_in.at[n])
        for n, (source, into) in enumerate(((w1_in, w1), (w2_in, w2), (cot_hbm, cot_in)))
    ]
    for load in loads:
        load.start()
    lax.fori_loop(1, n_dev, greet, 0)

    def stack_forward(w, into):
        def step(i, carry):
            rows = pl.ds(pl.multiple_of(i * ch, ch), ch)
            into[rows, :] = jnp.concatenate([w[3 * i + t] for t in range(3)], axis=1)
            return carry

        lax.fori_loop(0, 9, step, 0)

    def stack_backward(w, into):
        def step(i, carry):
            rows = pl.ds(pl.multiple_of(i * ch, ch), ch)
            into[rows, :] = jnp.concatenate(
                [w[26 - 3 * i - t].astype(F32).T.astype(BF16) for t in range(3)], axis=1
            )
            return carry

        lax.fori_loop(0, 9, step, 0)

    def near(dx, dz):
        x, z = xy + dx, gz + dz
        there = (x >= 0) & (x < n_xy) & (z >= 0) & (z < n_gz)
        return there, (z, x)

    def landing(e, side):
        dx, dz = SIDES[side]
        if dz != 0:
            return tile_in.at[e, side - 2]
        return {0: grid_in, 4: mask_halo}[e].at[side] if e in (0, 4) else plane_in.at[e - 2, side]

    def halo_copy(e, side):
        dx, dz = SIDES[side]
        there, target = near(dx, dz)
        if e == 0 and dz == 0:
            source = grid
        elif e == 4:
            source = mask_out
        elif dz == 0:
            source = planes.at[e - 2, 1 if dx > 0 else 0]
        else:
            source = tile_out.at[e, 1 if dz > 0 else 0]
        return there, pltpu.make_async_remote_copy(
            src_ref=source,
            dst_ref=landing(e, side),
            send_sem=sem_halo.at[0, e, side],
            recv_sem=sem_halo.at[1, e, side],
            device_id=target,
            device_id_type=MESH,
        )

    for side, (dx, dz) in enumerate(SIDES):
        has_source, _ = near(-dx, -dz)

        @pl.when(jnp.logical_not(has_source))
        def _():
            for e in [e for e in range(5) if side in USED[e]]:
                ref = landing(e, side)
                ref[...] = jnp.zeros(ref.shape, BF16)

    dpad[...] = jnp.zeros(dpad.shape, BF16)
    slots = got.shape[0] * got.shape[1]
    cap = got.shape[1]
    slot = lax.broadcasted_iota(jnp.int32, (1, slots), 1)
    to_slot = lax.broadcasted_iota(jnp.int32, (n_dev, slots), 0) == slot // cap
    counts = jnp.broadcast_to(count[...].astype(F32), (8, n_dev)).astype(BF16)
    counts = dot(counts, jnp.where(to_slot, 1.0, 0.0).astype(BF16))[:1]
    live = lax.rem(slot, cap).astype(F32) < counts
    sent = jnp.concatenate(
        [
            jnp.where(live, feat[0].astype(F32), 0.0),
            jnp.broadcast_to(cell[...].astype(F32), (8, slots)),
            jnp.zeros((LANES - ch - 8, slots), F32),
        ],
        axis=0,
    )
    src[...] = sent.T.astype(BF16).reshape(src.shape)
    for i in range(4):
        wup[i * ch : (i + 1) * ch, :] = jnp.concatenate([w_up[2 * i], w_up[2 * i + 1]], axis=1)
    mask_out[...] = jnp.concatenate([mask_in[0], mask_in[1]], axis=0).astype(F32).astype(BF16)
    loads[0].wait()
    stack_forward(w1, a1)
    pl.semaphore_wait(barrier, n_dev - 1)

    def exchange(source, landed, sems):
        def copy(k):
            to = lax.rem(me + k, n_dev)
            return pltpu.make_async_remote_copy(
                src_ref=source(to),
                dst_ref=landed.at[me],
                send_sem=sems.at[0],
                recv_sem=sems.at[1],
                device_id=(lax.div(to, n_xy), lax.rem(to, n_xy)),
                device_id_type=MESH,
            )

        def finish():
            others = landed.at[pl.ds(0, n_dev - 1)]
            pltpu.make_async_copy(others, others, sems.at[0]).wait()
            pltpu.make_async_copy(others, others, sems.at[1]).wait()

        return copy, finish

    to_copy, to_finish = exchange(lambda to: src.at[to], got, sem_to)
    back_copy, back_finish = exchange(lambda to: slot_grad.at[to], ret, sem_back)
    gather_copy, gather_finish = exchange(lambda to: full_c.at[me], full_c, sem_c)

    def each_device(action):
        def step(k, carry):
            action(k)
            return carry

        lax.fori_loop(1, n_dev, step, 0)

    each_device(lambda k: to_copy(k).start())
    for side in USED[4]:
        there, copy = halo_copy(4, side)
        pl.when(there)(copy.start)
    got[me] = src[me]
    loads[1].wait()
    stack_forward(w2, a2)
    loads[2].wait()
    to_finish()

    listed = got[...].reshape(slots, LANES)
    half = 4 * LANES
    cells = listed[:, ch : ch + 1].astype(F32)
    owner = lax.broadcasted_iota(jnp.int32, (1, half // 2), 1).astype(F32)
    hot = jnp.where(cells == owner, 1.0, 0.0).astype(BF16)
    grid[...] = dot_tn(listed, hot)[:ch].astype(BF16)
    for side in (0, 1):
        there, copy = halo_copy(0, side)
        pl.when(there)(copy.start)
    column = lax.broadcasted_iota(jnp.int32, (1, half), 1)
    even = lax.rem(column, 2) == 0
    twice = jnp.where(
        lax.broadcasted_iota(jnp.int32, (LANES, 2 * LANES), 0)
        == lax.broadcasted_iota(jnp.int32, (LANES, 2 * LANES), 1) // 2,
        1.0,
        0.0,
    ).astype(BF16)

    def by_parity_of(values):
        wide = jnp.concatenate([dot(values[:, :LANES], twice), dot(values[:, LANES:], twice)], axis=1)
        none = jnp.zeros_like(wide)
        return jnp.concatenate(
            [jnp.where(even, wide, none), jnp.where(even, none, wide)], axis=0
        ).astype(BF16)

    def mask_row(tile, x):
        return jnp.concatenate([tile[x * ny + y : x * ny + y + 1] for y in range(ny)], axis=1)

    def lift(listed_parents, tile):
        up = dot(wup[...], listed_parents)
        result = []
        for a in range(2):
            pieces = []
            for y in range(ny):
                row = (2 * a + y % 2) * ch
                pieces.append(up[row : row + ch, (y // 2) * LANES : (y // 2 + 1) * LANES])
            result.append((jnp.concatenate(pieces, axis=1) * mask_row(tile, a)).astype(BF16))
        return result

    parents = by_parity_of(grid[...])
    own_mask = mask_out[...].astype(F32)

    lane = lax.broadcasted_iota(jnp.int32, (1, LANES), 1)

    def block(value, y):
        return value[:, y * LANES : (y + 1) * LANES]

    def plane_mask(x):
        return mask_row(own_mask, x)

    def cot_plane(x):
        return cot_in[:, x].astype(F32).reshape(ch, width)

    def send_planes(e, fields):
        for x in range(2):
            planes[e - 2, x] = fields[x]
        for side in (0, 1):
            there, copy = halo_copy(e, side)
            pl.when(there)(copy.start)

    def send_edges(e, fields, shift):
        period = len(fields) * ny
        edge = lax.rem(lane, period)
        first = jnp.zeros((ch, LANES), F32)
        last = jnp.zeros((ch, LANES), F32)
        for x, field in enumerate(fields):
            wide = field.astype(F32)
            for y in range(ny):
                here = edge == (shift + x * ny + y) % period
                part = block(wide, y)
                first = jnp.where(here, part[:, :1], first)
                last = jnp.where(here, part[:, LANES - 1 :], last)
        tile_out[e, 0] = first.astype(BF16)
        tile_out[e, 1] = last.astype(BF16)
        for side in (3, 6, 2, 4, 5, 7):
            if side in USED[e]:
                there, copy = halo_copy(e, side)
                pl.when(there)(copy.start)

    def arrive(e, sides):
        for side in sides:
            dx, dz = SIDES[side]
            has_source, _ = near(-dx, -dz)
            _, copy = halo_copy(e, side)
            pl.when(has_source)(copy.wait_recv)

    def tile(e, side):
        return tile_in[e, side - 2].astype(F32)

    def spread(held, xp, field, low, high):
        wide = field.astype(F32)
        held[xp, ch : 2 * ch, :] = field
        for y in range(ny):
            part = block(wide, y)
            at = xp * ny + y
            left = jnp.where(lane == 0, low[:, at : at + 1], pltpu.roll(part, 1, 1))
            right = jnp.where(
                lane == LANES - 1, high[:, at : at + 1], pltpu.roll(part, LANES - 1, 1)
            )
            cols = slice(y * LANES, (y + 1) * LANES)
            held[xp, 0:ch, cols] = left.astype(BF16)
            held[xp, 2 * ch : 3 * ch, cols] = right.astype(BF16)

    def reach(xp, count):
        return [ox for ox in (-1, 0, 1) if 0 <= xp - 1 - ox < count]

    def add(matrix, held, xp, count):
        steps = reach(xp, count)
        low = 3 * ch * (steps[0] + 1)
        product = dot(matrix[low : low + 3 * ch * len(steps), :], held[xp])
        for n, ox in enumerate(steps):
            x = xp - 1 - ox
            for oy in (-1, 0, 1):
                row = (3 * n + oy + 1) * ch
                cols = slice((1 - oy) * LANES, (1 - oy) * LANES + width)
                acc[x, :, cols] += product[row : row + ch]

    def result(count):
        return [acc[x, :, LANES : LANES + width] for x in range(count)]

    def conv(e, fields, held, matrix, meanwhile=()):
        acc[...] = jnp.zeros(acc.shape, F32)
        arrive(e, (3, 6))
        low, high = tile(e, 3), tile(e, 6)
        for xp in (1, 2):
            spread(held, xp, fields[xp - 1], low, high)
            add(matrix, held, xp, 2)
        arrive(e, (0, 4, 7))
        spread(held, 0, plane_in[e - 2, 0], tile(e, 4), tile(e, 7))
        add(matrix, held, 0, 2)
        for action in meanwhile:
            action()
        arrive(e, (1, 2, 5))
        spread(held, 3, plane_in[e - 2, 1], tile(e, 2), tile(e, 5))
        add(matrix, held, 3, 2)
        return result(2)

    def tap_sums(deltas, held, start):
        for x in range(2):
            dpad[x, :, LANES : LANES + width] = deltas[x]
        total = [jnp.zeros((3 * ch, 3 * ch), F32) for _ in range(3)]
        for xp in range(4):
            steps = reach(xp, 2)
            rows = [
                dpad[xp - 1 - ox, :, (1 - oy) * LANES : (1 - oy) * LANES + width]
                for ox in steps
                for oy in (-1, 0, 1)
            ]
            product = dot_nt(jnp.concatenate(rows, axis=0), held[start + xp])
            for n, ox in enumerate(steps):
                total[ox + 1] = total[ox + 1] + product[3 * ch * n : 3 * ch * (n + 1)]
        return [total[i // 3][(i % 3) * ch : (i % 3 + 1) * ch] for i in range(9)]

    def pack_taps(taps, pack):
        for i in range(9):
            pack[i * ch : (i + 1) * ch, :] = taps[i][:, :LANES]
        for i in range(5):
            second = taps[2 * i + 1][:, LANES:] if i < 4 else jnp.zeros((ch, ch), F32)
            row = (9 + i) * ch
            pack[row : row + ch, :] = jnp.concatenate([taps[2 * i][:, LANES:], second], axis=1)

    class Reduce:
        def __init__(self, pack, wire, in_gz, part, mid, in_xy, full, sems):
            self.pack, self.wire, self.in_gz, self.part = pack, wire, in_gz, part
            self.mid, self.in_xy, self.full, self.sems = mid, in_xy, full, sems
            self.rows = pack.shape[0] // n_gz
            self.sub = self.rows // n_xy

        def copies(self, phase):
            result = []
            for k in range(1, n_gz if phase in (0, 3) else n_xy):
                if phase in (0, 3):
                    to = lax.rem(gz + k, n_gz)
                    target = (to, xy)
                else:
                    to = lax.rem(xy + k, n_xy)
                    target = (gz, to)
                source, landed = [
                    lambda: (self.wire.at[to], self.in_gz.at[k - 1]),
                    lambda: (self.mid.at[to], self.in_xy.at[k - 1]),
                    lambda: (self.full.at[gz, xy], self.full.at[gz, xy]),
                    lambda: (self.full.at[gz], self.full.at[gz]),
                ][phase]()
                result.append(
                    pltpu.make_async_remote_copy(
                        src_ref=source,
                        dst_ref=landed,
                        send_sem=self.sems.at[0, phase, k - 1],
                        recv_sem=self.sems.at[1, phase, k - 1],
                        device_id=target,
                        device_id_type=MESH,
                    )
                )
            return result

        def start(self, phase):
            for copy in self.copies(phase):
                copy.start()

        def finish(self, phase):
            for copy in self.copies(phase):
                copy.wait()

        def begin(self):
            for g in range(n_gz):
                self.wire[g] = self.pack[g * self.rows : (g + 1) * self.rows].astype(BF16)
            self.start(0)

        def second(self):
            self.finish(0)
            total = self.pack[pl.ds(pl.multiple_of(gz * self.rows, 16), self.rows), :]
            for k in range(n_gz - 1):
                total = total + self.in_gz[k].astype(F32)
            for j in range(n_xy):
                piece = total[j * self.sub : (j + 1) * self.sub]
                self.part[j] = piece
                self.mid[j] = piece.astype(BF16)
            self.start(1)

        def third(self):
            self.finish(1)
            total = self.part[xy]
            for k in range(n_xy - 1):
                total = total + self.in_xy[k].astype(F32)
            self.full[gz, xy] = total.astype(BF16)
            self.start(2)

        def fourth(self):
            self.finish(2)
            self.start(3)

        def done(self):
            self.finish(3)
            return self.full[...].reshape(self.rows * n_gz, LANES)

    sum_a = Reduce(pack_a, wire_a, in_a, part_a, mid_a, inx_a, full_a, sem_ra)
    sum_b = Reduce(pack_b, wire_b, in_b, part_b, mid_b, inx_b, full_b, sem_rb)

    lifted = lift(parents, own_mask)
    send_edges(0, lifted, 0)
    stack_backward(w2, b2)
    acc[...] = jnp.zeros(acc.shape, F32)
    arrive(0, (3, 6))
    low, high = tile(0, 3), tile(0, 6)
    for x in range(2):
        spread(s_lift, x + 2, lifted[x], low, high)
        add(a1, s_lift, x + 2, 4)
    around = []
    for side in (0, 1):
        arrive(4, (side,))
        arrive(0, (0, 4, 7) if side == 0 else (1, 2, 5))
        around.append(mask_halo[side].astype(F32))
        beside = lift(by_parity_of(grid_in[side]), around[side])
        low, high = (tile(0, 4), tile(0, 7)) if side == 0 else (tile(0, 2), tile(0, 5))
        for x in range(2):
            xp = 4 * side + x
            spread(s_lift, xp, beside[x], low, high)
            add(a1, s_lift, xp, 4)
    first = result(4)
    rows = [mask_row(around[0], 1), plane_mask(0), plane_mask(1), mask_row(around[1], 0)]
    acts = [(rows[x] * first[x] * jax.nn.sigmoid(first[x])).astype(BF16) for x in range(4)]
    send_edges(1, acts, 0)
    stack_backward(w1, b1)
    for x in range(2):
        pre1[x] = first[x + 1]
    acc[...] = jnp.zeros(acc.shape, F32)
    arrive(1, (3, 6))
    low, high = tile(1, 3), tile(1, 6)
    for xp in range(4):
        spread(s_act, xp, acts[xp], low, high)
        add(a2, s_act, xp, 2)
    second = result(2)
    deltas = []
    for x in range(2):
        v = second[x]
        sig = jax.nn.sigmoid(v)
        m = plane_mask(x)
        dec[:, x * width : (x + 1) * width] = (m * (v * sig)).astype(BF16)
        slope = sig * (1.0 + v * (1.0 - sig))
        deltas.append((cot_plane(x) * m * slope).astype(BF16))

    used = 14 * ch
    for pack in (pack_a, pack_b):
        if pack.shape[0] > used:
            pack[used:, :] = jnp.zeros((pack.shape[0] - used, LANES), F32)
    send_planes(2, deltas)
    send_edges(2, deltas, 8)
    pack_taps(tap_sums(deltas, s_act, 0), pack_a)
    sum_a.begin()
    back = conv(2, deltas, s_grad, b2, (sum_a.second,))
    deltas = []
    for x in range(2):
        v = pre1[x]
        sig = jax.nn.sigmoid(v)
        slope = sig * (1.0 + v * (1.0 - sig))
        deltas.append((back[x] * plane_mask(x) * slope).astype(BF16))
    send_planes(3, deltas)
    send_edges(3, deltas, 8)
    pack_taps(tap_sums(deltas, s_lift, 1), pack_b)
    sum_b.begin()
    sum_a.third()
    back = conv(3, deltas, s_grad, b1, (sum_b.second, sum_a.fourth))
    du = [(back[x] * plane_mask(x)).astype(BF16) for x in range(2)]
    stacked = jnp.concatenate(
        [
            jnp.concatenate([block(du[a], 2 * j + b) for j in range(ny // 2)], axis=1)
            for a in range(2)
            for b in range(2)
        ],
        axis=0,
    )
    grad_up = dot_nt(stacked, parents)
    by_parity = dot_tn(wup[...], stacked)
    kept = jnp.where(even, by_parity[:ch], by_parity[ch:])
    paired = kept + pltpu.roll(kept, half - 1, 1)
    parent_grad = jnp.where(even, paired, jnp.zeros_like(paired)).astype(BF16)
    compact = jnp.concatenate(
        [dot_nt(parent_grad[:, h * 2 * LANES : (h + 1) * 2 * LANES], twice) for h in range(2)],
        axis=1,
    )
    compact = jnp.concatenate([compact, jnp.zeros_like(compact)], axis=0).astype(BF16)
    terms = jnp.concatenate([grad_up[:, :ch], grad_up[:, ch:]], axis=0)
    if slots > 8 * ch:
        terms = jnp.concatenate([terms, jnp.zeros((slots - 8 * ch, ch), F32)], axis=0)
    both = jnp.concatenate([dot_nt(hot, compact)[:, :ch], terms], axis=1)
    slot_grad[...] = both.astype(BF16).reshape(slot_grad.shape)
    each_device(lambda k: back_copy(k).start())
    ret[me] = slot_grad[me]
    sum_b.third()
    back_finish()
    sum_b.fourth()
    total = ret[0].astype(F32)
    for d in range(1, n_dev):
        total = total + ret[d].astype(F32)
    full_c[me] = total.astype(BF16)
    each_device(lambda k: gather_copy(k).start())
    returned = ret[...].reshape(slots, LANES).astype(F32).T[:ch]
    ret_out[...] = jnp.where(live, returned, 0.0).astype(BF16)
    out_a[...] = sum_a.done()
    gather_finish()
    out_c[...] = full_c[...].reshape(out_c.shape)
    out_b[...] = sum_b.done()
    for e in range(5):
        for side in USED[e]:
            there, copy = halo_copy(e, side)
            pl.when(there)(copy.wait_send)


def finish_kernel(scale, dims, dec, ret, full_a, full_b, full_c, dec_out, ret_out, g1_out, g2_out, gup_out):
    ch, ny = dims
    width = ny * LANES
    for x in range(2):
        plane = dec[:, x * width : (x + 1) * width].astype(F32)
        dec_out[:, x] = plane.reshape(ch, ny, LANES).astype(BF16)
    ret_out[0] = ret[...]
    for full, out in ((full_b, g1_out), (full_a, g2_out)):
        for i in range(9):
            tile = full[i * ch : (i + 1) * ch].astype(F32) * scale
            out[3 * i] = tile[:, :ch]
            out[3 * i + 1] = tile[:, ch:]
            pair = full[(9 + i // 2) * ch : (10 + i // 2) * ch].astype(F32) * scale
            out[3 * i + 2] = pair[:, :ch] if i % 2 == 0 else pair[:, ch:]
    for p in range(4):
        for e in range(2):
            row = (4 * e + p) * ch
            gup_out[2 * p + e] = full_c[row : row + ch].astype(F32)[:, ch:] * scale


def local(
    parent_feat, parent_cell, send_count, up_weight, conv_one, conv_two, child_mask, cotangent
):
    ch, size_x, ny, size_z = cotangent.shape
    n_gz, n_xy = lax.axis_size("gz"), lax.axis_size("xy")
    n_dev = n_gz * n_xy
    slot_total = parent_feat.shape[2]
    cap = slot_total // n_dev
    voxels = size_x * ny * size_z
    width = ny * size_z
    unit = n_dev * 16
    rows_a = -(-14 * ch // unit) * unit
    assert 8 * ch <= slot_total

    def reduce_scratch(rows):
        per = rows // n_gz
        sub = per // n_xy
        return [
            pltpu.VMEM((rows, LANES), F32),
            pltpu.VMEM((n_gz, per, LANES), BF16),
            pltpu.VMEM((n_gz - 1, per, LANES), BF16),
            pltpu.VMEM((n_xy, sub, LANES), F32),
            pltpu.VMEM((n_xy, sub, LANES), BF16),
            pltpu.VMEM((n_xy - 1, sub, LANES), BF16),
            pltpu.VMEM((n_gz, n_xy, sub, LANES), BF16),
        ]

    vmem = pl.BlockSpec(memory_space=pltpu.VMEM)
    most = max(n_gz, n_xy) - 1
    dma = pltpu.SemaphoreType.DMA
    dec, ret, full_a, full_b, full_c = pl.pallas_call(
        functools.partial(all_kernel, (n_gz, n_xy, ch, ny)),
        out_shape=(
            jax.ShapeDtypeStruct((ch, voxels), BF16),
            jax.ShapeDtypeStruct((ch, slot_total), BF16),
            jax.ShapeDtypeStruct((rows_a, LANES), BF16),
            jax.ShapeDtypeStruct((rows_a, LANES), BF16),
            jax.ShapeDtypeStruct((slot_total, LANES), BF16),
        ),
        in_specs=[vmem] * 4 + [pl.BlockSpec(memory_space=pl.ANY)] * 2 + [vmem, pl.BlockSpec(memory_space=pl.ANY)],
        out_specs=(vmem,) * 5,
        scratch_shapes=[
            pltpu.VMEM(conv_one.shape, BF16),
            pltpu.VMEM(conv_two.shape, BF16),
            pltpu.VMEM(cotangent.shape, BF16),
            dma((3,)),
            pltpu.VMEM((n_dev, cap, LANES), BF16),
            pltpu.VMEM((4 * ch, 2 * ch), BF16),
            pltpu.VMEM((n_dev, cap, LANES), BF16),
            pltpu.VMEM((n_dev, cap, LANES), BF16),
            pltpu.VMEM((n_dev, cap, LANES), BF16),
            pltpu.VMEM((9 * ch, 3 * ch), BF16),
            pltpu.VMEM((9 * ch, 3 * ch), BF16),
            pltpu.VMEM((9 * ch, 3 * ch), BF16),
            pltpu.VMEM((9 * ch, 3 * ch), BF16),
            pltpu.VMEM((ch, 2 * LANES), BF16),
            pltpu.VMEM((2, ch, 2 * LANES), BF16),
            pltpu.VMEM((2 * ny, LANES), BF16),
            pltpu.VMEM((2, 2 * ny, LANES), BF16),
            pltpu.VMEM((2, 2, ch, width), BF16),
            pltpu.VMEM((2, 2, ch, width), BF16),
            pltpu.VMEM((4, 2, ch, LANES), BF16),
            pltpu.VMEM((4, 6, ch, LANES), BF16),
            pltpu.VMEM((6, 3 * ch, width), BF16),
            pltpu.VMEM((4, 3 * ch, width), BF16),
            pltpu.VMEM((4, 3 * ch, width), BF16),
            pltpu.VMEM((4, ch, width + 2 * LANES), F32),
            pltpu.VMEM((2, ch, width + 2 * LANES), BF16),
            pltpu.VMEM((2, ch, width), F32),
            *reduce_scratch(rows_a),
            *reduce_scratch(rows_a),
            pltpu.VMEM((n_dev, cap, LANES), BF16),
            dma((2,)),
            dma((2,)),
            dma((2, 5, 8)),
            dma((2, 4, most)),
            dma((2, 4, most)),
            dma((2,)),
        ],
        compiler_params=pltpu.CompilerParams(
            collective_id=0, has_side_effects=True, vmem_limit_bytes=56 * 1024 * 1024
        ),
    )(parent_feat, parent_cell, send_count, up_weight, conv_one, conv_two, child_mask, cotangent)
    scale = 1.0 / math.sqrt(size_x * n_xy * ny * size_z * n_gz)
    return pl.pallas_call(
        functools.partial(finish_kernel, scale, (ch, ny)),
        out_shape=(
            jax.ShapeDtypeStruct(cotangent.shape, BF16),
            jax.ShapeDtypeStruct((1, ch, slot_total), BF16),
            jax.ShapeDtypeStruct((27, ch, ch), F32),
            jax.ShapeDtypeStruct((27, ch, ch), F32),
            jax.ShapeDtypeStruct((8, ch, ch), F32),
        ),
        in_specs=[vmem] * 5,
        out_specs=(vmem,) * 5,
    )(dec, ret, full_a, full_b, full_c)


def solution(mesh):
    placed = (
        P(("gz", "xy"), None, None),
        P(("gz", "xy"), None),
        P(("gz", "xy"), None),
        P(),
        P(),
        P(),
        P("xy", None, "gz"),
        P(None, "xy", None, "gz"),
    )
    return jax.shard_map(
        local,
        mesh=mesh,
        in_specs=placed,
        out_specs=(P(None, "xy", None, "gz"), P(("gz", "xy"), None, None), P(), P(), P()),
        check_vma=False,
    )
```
